512 devices in a mesh: segment: 16 (over z_lo, core), db: 16 (over x, y), mp: 2 (over z_hi).
Axes of the slice: x: 4, y: 4, z: 16 (z_hi: 2, z_lo: 8; z = z_hi * 8 + z_lo), core: 2. Of those that a mesh axis runs over, the one named last changes fastest.
Arguments:
- stream: bfloat16 [16, 6144, 4096], P('segment', 'db', 'mp'), may hold values from -6 to 6
- gain: float32 [16, 4096], P('segment', 'mp'), may hold values from 0.25 to 150
- key_weight: bfloat16 [16, 448, 4096], P('segment', 'db', 'mp'), may hold values from -0.25 to 0.25
- value_weight: bfloat16 [16, 448, 4096], P('segment', 'db', 'mp'), may hold values from -0.25 to 0.25
- owners: int32 [16, 96, 2], P('segment', 'db'), may hold values from 0 to 15, all different within a row; in each aligned block of 6 rows (0 to 5, 6 to 11, ..., all dimensions but the last counted through in order) at most 2 rows name the same one
- blocks: int32 [16, 96, 2], P('segment', 'db'), may hold values from 0 to 5
- valid: int32 [16, 96, 2], P('segment', 'db'), may hold values from 0 to 1, as said below
- database: bfloat16 [96, 128, 448], P('db'), may hold values from -6 to 6
Outputs:
- updated: bfloat16 [16, 6144, 4096], P('segment', 'db', 'mp')
The draws below stay inside these ranges and needn't reach their ends.
Inputs may be any that keep to these rules, and one draw needn't show every extreme that they name: In the 6 groups that one index of db holds of one micro-batch, no owner is named by more than 2 neighbours; the 2 neighbours of a group have different owners. `valid`: 0 or 1; both neighbours of the first group of each 2048-token sequence are 0.
All inputs are finite; a program needn't handle non-finite values.
Results may differ from the reference program's by a relative error of at most 0.0045.
The reference program's roundings to bfloat16 on the way count: a program that leaves them out, or rounds other values in their place, can miss the bound.
Values may be sent and summed in bfloat16 or wider, within the bound.
No kernel may reach another device: no remote copies, remote signals or barrier semaphores. Data moves between devices by JAX's collectives and lax.ppermute only.
A program may use at most 128 MiB of HBM per device.

```python
import math
import jax
import jax.numpy as jnp
import numpy as np
from jax import lax

HEADS = 32
HD = 128
ENC = 448
GROUP = 64
NEIGH = 2
BLOCK = 128
LENGTH = 2048
BLOCKS_DEV = 6
WIDTH = 4096
GROUPS_DEV = 6
TOKENS = 6144
DBLOCKS = 96
CAP = 2
N_SEGMENT = 16
N_DB = 16


def draw_gain(key, part):
    key = jax.random.fold_in(key, 5)
    key_base = jax.random.fold_in(key, 0)
    channel_gain = jnp.exp(jax.random.uniform(key_base, (N_SEGMENT, WIDTH), jnp.float32, math.log(0.25), math.log(4.0)))
    return jnp.clip(channel_gain, 0.25, 150.0).astype(jnp.float32)


def draw_valid(key, part):
    key = jax.random.fold_in(key, 11)
    groups = TOKENS // GROUP
    chosen = (jax.random.randint(key, (N_SEGMENT, groups, NEIGH), 0, 4) < 3).astype(jnp.int32)
    starts = jnp.arange(groups) % (LENGTH // GROUP) == 0
    return jnp.where(starts[None, :, None], 0, chosen).astype(jnp.int32)


def touch_ends(values, rng, least, largest):
    spot = [jax.random.randint(jax.random.fold_in(rng, axis), (), 0, length) for axis, length in enumerate(values.shape)]
    longest = values.shape.index(max(values.shape))
    next_to = spot[:longest] + [(spot[longest] + 1) % values.shape[longest]] + spot[longest + 1:]
    return values.at[tuple(spot)].set(least).at[tuple(next_to)].set(largest)


def block_scale(rng, shape, cuts, least, top_value):
    level, own = 1.0, jax.random.fold_in(rng, 6)
    for axis_at, blocks in cuts:
        heights = jnp.exp(jax.random.uniform(jax.random.fold_in(own, axis_at), (blocks,), jnp.float32, least / len(cuts), top_value / len(cuts)))
        level = level * jnp.repeat(heights, shape[axis_at] // blocks).reshape([-1 if axis == axis_at else 1 for axis in range(len(shape))])
    return level


def routed_block(own_key, own, number, rows, amount, top, reach, lean):
    order = jax.random.permutation(own_key, amount)
    packed, common = portions_of(amount, rows * top, reach, lean, True), portions_of(amount, rows * top, reach, lean, False)
    places = jnp.arange(amount)

    def named(sizes, turn):
        used = int((sizes > 0).sum())
        fixed = max(1, used // 4)
        moved = fixed + (places - fixed + turn * (used - fixed)) % max(1, amount - fixed)
        return jnp.zeros((amount,), jnp.int32).at[order[jnp.where(places < fixed, places, moved)]].set(jnp.asarray(sizes, jnp.int32))

    sizes = jnp.where(number % 4 == 0, named(packed, number // 4), named(common, number - number // 4 - 1))
    mixed = jax.random.permutation(jax.random.fold_in(own, 3), amount)
    source_of, taker = mixed[0:amount // 2 * 2:2], mixed[1:amount // 2 * 2:2]
    slack = jnp.minimum(sizes[source_of] - 1, reach - sizes[taker]) // 2
    slack = jnp.where((source_of == order[0]) | (taker == order[0]) | (sizes[taker] == 0), 0, jnp.maximum(slack, 0))
    moved = jax.random.randint(jax.random.fold_in(own, 4), (amount // 2,), 0, 1 << 20) % (slack + 1)
    sizes = sizes.at[source_of].add(-moved).at[taker].add(moved)
    members = jnp.searchsorted(jnp.cumsum(sizes), jnp.arange(rows * top), side="right").astype(jnp.int32)
    grid = members.reshape(top, rows).T
    grid = grid[jax.random.permutation(jax.random.fold_in(own, 1), rows)]
    turn = jax.random.randint(jax.random.fold_in(own, 2), (rows, 1), 0, top)
    return jnp.take_along_axis(grid, (jnp.arange(top)[None, :] + turn) % top, axis=1)


def portions_of(number_of, total, bound, skew, full):
    loads = [(1 << 20) // math.isqrt(rank ** skew) + 1 for rank in range(1, number_of + 1)]
    largest = bound if full else min(bound, max(-(-total // number_of), total * loads[0] // sum(loads)))
    least = 1 if total - largest >= number_of - 1 else 0
    counts, spare = [largest] + [least] * (number_of - 1), total - largest - least * (number_of - 1)
    while spare > 0:
        movable = [i for i in range(1, number_of) if counts[i] < largest] or [i for i in range(1, number_of) if counts[i] < bound]
        whole, remaining = sum([loads[i] for i in movable]), spare
        for i in movable:
            addition = min(bound - counts[i], max(1, remaining * loads[i] // whole), spare)
            counts[i] = counts[i] + addition
            spare = spare - addition
    return np.array(counts)


def scatter_about(stream_key, dims, width, reach, cuts=(), held_as=jnp.bfloat16):
    result = width * jax.random.normal(stream_key, dims, jnp.float32)
    if cuts:
        result = result * block_scale(stream_key, dims, cuts, -0.22, 0.18)
    return jnp.clip(result, -reach, reach).astype(held_as)


def setup_inputs(seed: int = 0) -> dict:
    seeds = jax.random.split(jax.random.key(seed), 9)
    stream = scatter_about(seeds[0], (N_SEGMENT, TOKENS, WIDTH), 1.0, 6.0, ((0, 16), (1, 16), (2, 2)))
    gain = draw_gain(jax.random.fold_in(seeds[8], 71), 0)
    key_weight = scatter_about(seeds[2], (N_SEGMENT, ENC, WIDTH), ENC ** -0.5, 0.25, ((0, 16), (1, 16), (2, 2)))
    value_weight = scatter_about(seeds[3], (N_SEGMENT, ENC, WIDTH), ENC ** -0.5, 0.25, ((0, 16), (1, 16), (2, 2)))
    owners_keys = jax.random.split(jax.random.fold_in(seeds[4], 1), N_SEGMENT * (TOKENS // GROUP) // GROUPS_DEV)
    owners_turns = jax.random.permutation(jax.random.fold_in(seeds[4], 3), N_SEGMENT * (TOKENS // GROUP) // GROUPS_DEV)
    owners = jax.vmap(lambda own, number: routed_block(jax.random.fold_in(seeds[4], 2), own, number, GROUPS_DEV, N_DB, NEIGH, CAP, 2))(owners_keys, owners_turns).reshape((N_SEGMENT, TOKENS // GROUP, NEIGH))
    blocks = touch_ends(jax.random.randint(seeds[5], (N_SEGMENT, TOKENS // GROUP, NEIGH), 0, BLOCKS_DEV), jax.random.fold_in(seeds[5], 1), 0, BLOCKS_DEV - 1).astype(jnp.int32)
    valid = draw_valid(jax.random.fold_in(seeds[8], 71), 0)
    database = scatter_about(seeds[7], (DBLOCKS, BLOCK, ENC), 1.0, 6.0, ((0, 16),))
    return dict(stream=stream, gain=gain, key_weight=key_weight, value_weight=value_weight, owners=owners, blocks=blocks, valid=valid, database=database)


eps_norm = 1e-06

def cross_section(stream_rows, gain_row, key_proj, value_proj, owner_ids, block_ids, valid_ids, database):
    as_float = stream_rows.astype(jnp.float32)
    mean_square = lax.optimization_barrier(jnp.sum(as_float * as_float, axis=1)) / WIDTH
    inv_rms = lax.rsqrt(mean_square + eps_norm)
    queries = (as_float * inv_rms[:, None] * gain_row[None, :] * HD ** (-0.5)).astype(jnp.bfloat16)
    groups = TOKENS // GROUP
    row_index = (owner_ids * BLOCKS_DEV + block_ids).reshape(-1).astype(jnp.int32)
    picked = jnp.take(database, row_index, axis=0).reshape(groups * NEIGH * BLOCK, ENC)
    key_block = jnp.dot(picked, key_proj, preferred_element_type=jnp.float32).astype(jnp.bfloat16)
    value_block = jnp.dot(picked, value_proj, preferred_element_type=jnp.float32).astype(jnp.bfloat16)
    query_heads = lax.optimization_barrier(queries).astype(jnp.float32).reshape(groups, GROUP, HEADS, HD)
    key_heads = lax.optimization_barrier(key_block).astype(jnp.float32).reshape(groups, NEIGH * BLOCK, HEADS, HD)
    value_heads = lax.optimization_barrier(value_block).astype(jnp.float32).reshape(groups, NEIGH * BLOCK, HEADS, HD)
    scores = jnp.einsum('cthd,cshd->chts', query_heads, key_heads)
    is_live = jnp.repeat(valid_ids > 0, BLOCK, axis=1)
    live_mask = is_live[:, None, None, :]
    row_max = lax.optimization_barrier(jnp.max(jnp.where(live_mask, scores, -1e+30), axis=3, keepdims=True))
    any_live = jnp.any(is_live, axis=1)[:, None, None, None]
    row_max = jnp.where(any_live, row_max, 0.0)
    shifted = jnp.where(live_mask, scores - row_max, -1e+30)
    expo = jnp.exp(shifted)
    row_total = jnp.maximum(lax.optimization_barrier(jnp.sum(expo, axis=3, keepdims=True)), 1.0)
    weights_bf = (expo / row_total).astype(jnp.bfloat16)
    weights_back = lax.optimization_barrier(weights_bf).astype(jnp.float32)
    attended = jnp.einsum('chts,cshd->cthd', weights_back, value_heads).reshape(TOKENS, WIDTH)
    return (as_float + attended).astype(jnp.bfloat16)

def reference(stream, gain, key_weight, value_weight, owners, blocks, valid, database):

    def one_segment(pieces):
        return cross_section(pieces[0], pieces[1], pieces[2], pieces[3], pieces[4], pieces[5], pieces[6], database)
    results = lax.map(one_segment, (stream, gain, key_weight, value_weight, owners, blocks, valid))
    return jnp.roll(results, 1, axis=0)
```

```python
import jax
import jax.numpy as jnp
from jax import lax
from jax.experimental import pallas as pl
from jax.experimental.pallas import tpu as pltpu
from jax.sharding import PartitionSpec as P

HD = 128
GROUP = 64
SIDE = 4
RING = SIDE * SIDE
eps_norm = 1e-06

W_PART = 28
W_PAD = 32
HEADS_HERE = 16
W_ROWS = HEADS_HERE * 2 * W_PAD
ENC = 448
ENC_PAD = RING * W_PAD
HALF = 64
TILES = 2 * ENC // HD
PAIRS = 3
D_ROWS = PAIRS * TILES * HALF
SLAB = ENC_PAD // HD * HALF
REQ = 12
HB = 2


def ring_pairs(segments, turn, along_x_core):
    pairs = []
    for seg in range(segments):
        for place in range(RING):
            x, y = divmod(place, SIDE)
            if seg % 2 == along_x_core:
                to = ((x + turn) % SIDE) * SIDE + y
            else:
                to = x * SIDE + (y + turn) % SIDE
            pairs.append((seg * RING + place, seg * RING + to))
    return pairs


def ring_groups(segments, along_x_core):
    groups = []
    for seg in range(segments):
        for line in range(SIDE):
            if seg % 2 == along_x_core:
                groups.append([seg * RING + x * SIDE + line for x in range(SIDE)])
            else:
                groups.append([seg * RING + line * SIDE + y for y in range(SIDE)])
    return groups


def turned(value, turn, along_x_core):
    pairs = ring_pairs(lax.axis_size("segment"), turn, along_x_core)
    return lax.ppermute(value, ("segment", "db"), pairs)


def to_next(value):
    count = lax.axis_size("segment")
    return lax.ppermute(value, "segment", [(s, (s + 1) % count) for s in range(count)])


def to_next_other_core(value):
    count = lax.axis_size("segment")
    return lax.ppermute(value, "segment", [(s, ((s + 1) % count) ^ 1) for s in range(count)])


def to_next_other_mp(value):
    count = lax.axis_size("segment")
    pairs = [(s * 2 + m, ((s + 1) % count) * 2 + 1 - m) for s in range(count) for m in range(2)]
    return lax.ppermute(value, ("segment", "mp"), pairs)


def other_core(value):
    count = lax.axis_size("segment")
    return lax.ppermute(value, "segment", [(s, s ^ 1) for s in range(count)])


def pick_kernel(table, c_ref, l_ref, r_ref, ol_ref, or_ref, s_own, s_other, own_out, other_out, slabs, sems):
    sources = (c_ref, l_ref, r_ref, ol_ref, or_ref)

    def begin(i, carry):
        which = table[0, i]
        row = pl.multiple_of(table[1, i], 64)
        for number, source in enumerate(sources):
            @pl.when(which == number)
            def _():
                pltpu.make_async_copy(source.at[pl.ds(row, SLAB)], slabs.at[i], sems.at[i]).start()
        return carry

    def finish(i, carry):
        pltpu.make_async_copy(c_ref.at[pl.ds(0, SLAB)], slabs.at[i], sems.at[i]).wait()
        return carry

    lax.fori_loop(0, 2 * REQ, begin, 0)
    for part, (spread, out) in enumerate(((s_own, own_out), (s_other, other_out))):
        lax.fori_loop(part * REQ, (part + 1) * REQ, finish, 0)
        rows = []
        for i in range(REQ):
            slab = slabs[part * REQ + i]
            rows.append(jnp.concatenate([slab[t * HALF:(t + 1) * HALF] for t in range(ENC_PAD // HD)], axis=1))
        stacked = jnp.concatenate(rows, axis=0)
        even = jnp.dot(stacked, spread[0], preferred_element_type=jnp.float32)
        odd = jnp.dot(stacked, spread[1], preferred_element_type=jnp.float32)
        for i in range(REQ):
            here = slice(i * HALF, (i + 1) * HALF)
            is_odd = table[2, part * REQ + i] == 1
            out[here] = jnp.where(is_odd, odd[here], even[here]).astype(jnp.bfloat16)


def pick(table, pieces, s_own, s_other):
    any_space = pl.BlockSpec(memory_space=pl.ANY)
    vmem = pl.BlockSpec(memory_space=pltpu.VMEM)
    shape = jax.ShapeDtypeStruct((REQ * HALF, ENC_PAD), jnp.bfloat16)
    return pl.pallas_call(
        pick_kernel,
        in_specs=[pl.BlockSpec(memory_space=pltpu.SMEM)] + [any_space] * 5 + [vmem] * 2,
        out_specs=[vmem] * 2,
        out_shape=[shape] * 2,
        scratch_shapes=[
            pltpu.VMEM((2 * REQ, SLAB, HD), jnp.bfloat16),
            pltpu.SemaphoreType.DMA((2 * REQ,)),
        ],
        compiler_params=pltpu.CompilerParams(vmem_limit_bytes=40 * 2**20),
        name="pick_encodings",
    )(table, *pieces, s_own, s_other)


def attend_kernel(live, own_ref, other_ref, w_ref, x_ref, inv_ref, gain_ref, out_ref):
    own, other = own_ref[...], other_ref[...]
    inv = inv_ref[...]
    groups = x_ref.shape[0] // GROUP
    column = lax.broadcasted_iota(jnp.int32, (1, HD), 1)
    masks = []
    for c in range(groups):
        first, second = live[2 * c], live[2 * c + 1]
        masks.append(jnp.where(column < HALF, first, second) > 0)
    for b in range(HB):
        base = b * 2 * W_PAD
        head = slice(b * HD, (b + 1) * HD)
        key_w = jnp.concatenate([w_ref[j, base:base + W_PAD] for j in range(RING)], axis=0)
        value_w = jnp.concatenate([w_ref[j, base + W_PAD:base + 2 * W_PAD] for j in range(RING)], axis=0)
        weight = jnp.concatenate([key_w, value_w], axis=1)
        kv_own = jnp.dot(own, weight, preferred_element_type=jnp.float32).astype(jnp.bfloat16)
        kv_other = jnp.dot(other, weight, preferred_element_type=jnp.float32).astype(jnp.bfloat16)
        x = x_ref[:, head].astype(jnp.float32)
        q = (x * inv * gain_ref[:, head] * HD ** (-0.5)).astype(jnp.bfloat16)
        for c in range(groups):
            rows = slice(c * GROUP, (c + 1) * GROUP)
            keys = slice(c * 2 * HALF, (c + 1) * 2 * HALF)
            key = jnp.concatenate([kv_own[keys, :HD], kv_other[keys, :HD]], axis=0)
            value = jnp.concatenate([kv_own[keys, HD:], kv_other[keys, HD:]], axis=0)
            scores = lax.dot_general(q[rows], key, (((1,), (1,)), ((), ())), preferred_element_type=jnp.float32)
            mask = jnp.concatenate([masks[c], masks[c]], axis=1)
            masked = jnp.where(mask, scores, -1e30)
            row_max = jnp.max(masked, axis=1, keepdims=True)
            row_max = jnp.where(row_max > -1e29, row_max, 0.0)
            expo = jnp.exp(masked - row_max)
            total = jnp.maximum(jnp.sum(expo, axis=1, keepdims=True), 1.0)
            probs = (expo * (1.0 / total)).astype(jnp.bfloat16)
            attended = jnp.dot(probs, value, preferred_element_type=jnp.float32)
            out_ref[rows, head] = (x[rows] + attended).astype(jnp.bfloat16)


def attend(live, own, other, weights, x, inv, gain):
    tokens, width = x.shape
    whole = lambda *shape: pl.BlockSpec(shape, lambda i, live: (0,) * len(shape))
    return pl.pallas_call(
        attend_kernel,
        grid_spec=pltpu.PrefetchScalarGridSpec(
            num_scalar_prefetch=1,
            grid=(HEADS_HERE // HB,),
            in_specs=[
                whole(REQ * HALF, ENC_PAD),
                whole(REQ * HALF, ENC_PAD),
                pl.BlockSpec((RING, HB * 2 * W_PAD, HD), lambda i, live: (0, i, 0)),
                pl.BlockSpec((tokens, HB * HD), lambda i, live: (0, i)),
                whole(tokens, 1),
                pl.BlockSpec((1, HB * HD), lambda i, live: (0, i)),
            ],
            out_specs=pl.BlockSpec((tokens, HB * HD), lambda i, live: (0, i)),
        ),
        out_shape=jax.ShapeDtypeStruct((tokens, width), jnp.bfloat16),
        compiler_params=pltpu.CompilerParams(vmem_limit_bytes=40 * 2**20),
        name="attend_heads",
    )(live, own, other, weights, x, inv, gain)


def spread_of(core, x, y):
    u = jnp.where(core == 0, x, y)
    channel = lax.broadcasted_iota(jnp.int32, (ENC_PAD, ENC_PAD), 0)
    column = lax.broadcasted_iota(jnp.int32, (ENC_PAD, ENC_PAD), 1)

    def put(source):
        owner, row = source // W_PART, source % W_PART
        ou = jnp.where(core == 0, owner // SIDE, owner % SIDE)
        ov = jnp.where(core == 0, owner % SIDE, owner // SIDE)
        place = (ov * SIDE + (ou - u) % SIDE) * W_PAD + row
        used = jnp.logical_and(source >= 0, source < ENC)
        return jnp.logical_and(used, place == column).astype(jnp.bfloat16)

    return jnp.stack([put(channel), put(channel - (ENC_PAD - ENC))])


def source_table(requests, core, x, y):
    u, v = jnp.where(core == 0, x, y), jnp.where(core == 0, y, x)
    owner, block = requests // 6, requests % 6
    ou = jnp.where(core == 0, owner // SIDE, owner % SIDE)
    ov = jnp.where(core == 0, owner % SIDE, owner // SIDE)
    k, far = (ou - u) % SIDE, (ov - v) % SIDE
    opposite = jnp.where(k < 2, 3, 4)
    which = jnp.where(far == 0, 0, jnp.where(far == 1, 2, jnp.where(far == 3, 1, opposite)))
    chunk = jnp.where(which == 4, k - 2, k)
    odd = block % 2
    row = chunk * D_ROWS + (block // 2) * (TILES * HALF) + odd * (TILES - ENC_PAD // HD) * HALF
    return jnp.stack([which, row, odd])


def on_device(stream, gain, key_weight, value_weight, owners, blocks, valid, database):
    segments = lax.axis_size("segment")
    core = lax.axis_index("segment") % 2
    place = lax.axis_index("db")
    x_at, y_at = place // SIDE, place % SIDE
    rows = stream[0]
    tokens, local_width = rows.shape
    full_width = local_width * lax.axis_size("mp")

    def pack_weight(w):
        return jnp.pad(w[0], ((0, W_PAD - W_PART), (0, 0)))

    packed_w = jnp.concatenate([pack_weight(key_weight), pack_weight(value_weight)], axis=0)
    packed_w = packed_w.reshape(2 * W_PAD, HEADS_HERE, HD).transpose(1, 0, 2).reshape(W_ROWS, HD)
    next_w = to_next(packed_w)

    as_float = rows.astype(jnp.float32)
    squares = jnp.sum(as_float * as_float, axis=1)
    requests = (owners[0] * 6 + blocks[0]).reshape(-1)
    info = jnp.concatenate(
        [squares, gain[0], valid[0].reshape(-1).astype(jnp.float32), requests.astype(jnp.float32)]
    )
    info = jnp.pad(info, (0, -info.shape[0] % 1024)).reshape(-1, HD)
    info_here = to_next(info).reshape(-1)
    squares_other = to_next_other_mp(squares.reshape(-1, HD)).reshape(-1)
    requests_other = to_next_other_core(requests)
    x_here = to_next(rows)

    half = lax.dynamic_slice(database, (0, core * HALF, 0), (2 * PAIRS, HALF, ENC))
    paired = jnp.concatenate([half[0::2], half[1::2]], axis=2)
    packed_d = paired.reshape(PAIRS, HALF, TILES, HD).transpose(0, 2, 1, 3).reshape(D_ROWS, HD)

    payload = jnp.concatenate([next_w, packed_d], axis=0)
    cut = payload.shape[0] // 2
    before, after = turned(payload, 1, 0), turned(payload, -1, 0)
    opposite = jnp.concatenate([turned(before[:cut], 1, 0), turned(after[cut:], -1, 0)], axis=0)
    line = (payload, after, opposite, before)
    line_w = jnp.concatenate([piece[:W_ROWS] for piece in line], axis=0)
    line_d = jnp.concatenate([piece[W_ROWS:] for piece in line], axis=0)

    all_w = lax.all_gather(
        line_w, ("segment", "db"), axis=0, tiled=True, axis_index_groups=ring_groups(segments, 1)
    ).reshape(RING, W_ROWS, HD)
    d_before, d_after = turned(line_d, 1, 1), turned(line_d, -1, 1)
    mid = line_d.shape[0] // 2
    far_before, far_after = turned(d_before[:mid], 1, 1), turned(d_after[mid:], -1, 1)

    squares_here = info_here[:tokens]
    gain_here = info_here[tokens:tokens + local_width]
    ints = info_here[tokens + local_width:tokens + local_width + 2 * REQ].astype(jnp.int32)
    live, requests_here = ints[:REQ], ints[REQ:]
    inv_rms = lax.rsqrt((squares_here + squares_other) / full_width + eps_norm)

    table = jnp.concatenate(
        [source_table(requests_here, core, x_at, y_at), source_table(requests_other, core, x_at, y_at)], axis=1
    )
    own, given = pick(
        table,
        (line_d, d_before, d_after, far_before, far_after),
        spread_of(core, x_at, y_at),
        spread_of(1 - core, x_at, y_at),
    )
    other = other_core(given)
    updated = attend(live, own, other, all_w, x_here, inv_rms[:, None], gain_here[None, :])
    return updated[None]


def solution(mesh):
    return jax.shard_map(
        on_device,
        mesh=mesh,
        in_specs=(
            P("segment", "db", "mp"),
            P("segment", "mp"),
            P("segment", "db", "mp"),
            P("segment", "db", "mp"),
            P("segment", "db", None),
            P("segment", "db", None),
            P("segment", "db", None),
            P("db", None, None),
        ),
        out_specs=P("segment", "db", "mp"),
        check_vma=False,
    )
```

```python
import jax
import jax.numpy as jnp
from jax import lax
from jax.experimental import pallas as pl
from jax.experimental.pallas import tpu as pltpu
from jax.sharding import PartitionSpec as P

HD = 128
GROUP = 64
SIDE = 4
RING = SIDE * SIDE
eps_norm = 1e-06

W_PART = 28
W_PAD = 32
HEADS_HERE = 16
W_ROWS = HEADS_HERE * 2 * W_PAD
ENC = 448
ENC_PAD = RING * W_PAD
HALF = 64
TILES = 2 * ENC // HD
PAIRS = 3
D_ROWS = PAIRS * TILES * HALF
SLAB = ENC_PAD // HD * HALF
REQ = 12
HB = 2


def ring_pairs(segments, turn, along_x_core):
    pairs = []
    for seg in range(segments):
        for place in range(RING):
            x, y = divmod(place, SIDE)
            if seg % 2 == along_x_core:
                to = ((x + turn) % SIDE) * SIDE + y
            else:
                to = x * SIDE + (y + turn) % SIDE
            pairs.append((seg * RING + place, seg * RING + to))
    return pairs


def ring_groups(segments, along_x_core):
    groups = []
    for seg in range(segments):
        for line in range(SIDE):
            if seg % 2 == along_x_core:
                groups.append([seg * RING + x * SIDE + line for x in range(SIDE)])
            else:
                groups.append([seg * RING + line * SIDE + y for y in range(SIDE)])
    return groups


def turned(value, turn, along_x_core):
    pairs = ring_pairs(lax.axis_size("segment"), turn, along_x_core)
    return lax.ppermute(value, ("segment", "db"), pairs)


def to_next_turned(value, turn):
    count = lax.axis_size("segment")
    behind = ring_pairs(count, turn, 0)
    pairs = [(((seg - 1) % count) * RING + place, to) for seg in range(count) for place, to in
             [(source % RING, target) for source, target in behind[seg * RING:(seg + 1) * RING]]]
    return lax.ppermute(value, ("segment", "db"), pairs)


def to_next(value):
    count = lax.axis_size("segment")
    return lax.ppermute(value, "segment", [(s, (s + 1) % count) for s in range(count)])


def to_next_other_core(value):
    count = lax.axis_size("segment")
    return lax.ppermute(value, "segment", [(s, ((s + 1) % count) ^ 1) for s in range(count)])


def other_mp(value):
    return lax.ppermute(value, "mp", [(0, 1), (1, 0)])


def other_core(value):
    count = lax.axis_size("segment")
    return lax.ppermute(value, "segment", [(s, s ^ 1) for s in range(count)])


def fetch(table, first, sources, slabs, sems):
    def begin(i, carry):
        which = table[0, first + i]
        row = pl.multiple_of(table[1, first + i], 64)
        for number, source in enumerate(sources):
            @pl.when(which == number)
            def _():
                pltpu.make_async_copy(source.at[pl.ds(row, SLAB)], slabs.at[i], sems.at[i]).start()
        return carry

    def finish(i, carry):
        pltpu.make_async_copy(sources[0].at[pl.ds(0, SLAB)], slabs.at[i], sems.at[i]).wait()
        return carry

    lax.fori_loop(0, REQ, begin, 0)
    lax.fori_loop(0, REQ, finish, 0)


def spread_slabs(table, slabs, spread):
    tiles = ENC_PAD // HD
    rows = []
    for i in range(REQ):
        slab = slabs[i]
        rows.append(jnp.concatenate([slab[t * HALF:(t + 1) * HALF] for t in range(tiles)], axis=1))
    stacked = jnp.concatenate(rows, axis=0)
    even = jnp.dot(stacked, spread[0], preferred_element_type=jnp.float32)
    odd = jnp.dot(stacked, spread[1], preferred_element_type=jnp.float32)
    placed = []
    for i in range(REQ):
        here = slice(i * HALF, (i + 1) * HALF)
        placed.append(jnp.where(table[2, i] == 1, odd[here], even[here]).astype(jnp.bfloat16))
    return placed


def give_kernel(table, c_ref, r_ref, ol_ref, or_ref, l_ref, out_ref, sems):
    fetch(table, REQ, (c_ref, r_ref, ol_ref, or_ref, l_ref), out_ref, sems)


def pick_kernel(table, c_ref, r_ref, ol_ref, or_ref, l_ref, spread, out_ref, slabs, sems):
    fetch(table, 0, (c_ref, r_ref, ol_ref, or_ref, l_ref), slabs, sems)
    for i, block in enumerate(spread_slabs(table, slabs, spread)):
        out_ref[i * HALF:(i + 1) * HALF] = block


SMEM = pl.BlockSpec(memory_space=pltpu.SMEM)
VMEM = pl.BlockSpec(memory_space=pltpu.VMEM)
ANY = pl.BlockSpec(memory_space=pl.ANY)


def give(table, pieces):
    return pl.pallas_call(
        give_kernel,
        in_specs=[SMEM] + [ANY] * 5,
        out_specs=VMEM,
        out_shape=jax.ShapeDtypeStruct((REQ, SLAB, HD), jnp.bfloat16),
        scratch_shapes=[pltpu.SemaphoreType.DMA((REQ,))],
        compiler_params=pltpu.CompilerParams(vmem_limit_bytes=16 * 2**20),
        name="give_encodings",
    )(table, *pieces)


def pick(table, pieces, spread):
    return pl.pallas_call(
        pick_kernel,
        in_specs=[SMEM] + [ANY] * 5 + [VMEM],
        out_specs=VMEM,
        out_shape=jax.ShapeDtypeStruct((REQ * HALF, ENC_PAD), jnp.bfloat16),
        scratch_shapes=[
            pltpu.VMEM((REQ, SLAB, HD), jnp.bfloat16),
            pltpu.SemaphoreType.DMA((REQ,)),
        ],
        compiler_params=pltpu.CompilerParams(vmem_limit_bytes=32 * 2**20),
        name="pick_encodings",
    )(table, *pieces, spread)


def attend_kernel(
    live, table, own_ref, slabs, spread, w_ref, x_ref, inv_ref, gain_ref, out_ref, other_ref
):

    @pl.when(pl.program_id(0) == 0)
    def _():
        for i, block in enumerate(spread_slabs(table, slabs, spread)):
            other_ref[i * HALF:(i + 1) * HALF] = block

    own, other = own_ref[...], other_ref[...]
    inv = inv_ref[...]
    groups = x_ref.shape[0] // GROUP
    column = lax.broadcasted_iota(jnp.int32, (1, HD), 1)
    biases = []
    for c in range(groups):
        bias = jnp.where(jnp.where(column < HALF, live[2 * c], live[2 * c + 1]) > 0, 0.0, -1e30)
        biases.append(jnp.broadcast_to(jnp.concatenate([bias, bias], axis=1), (GROUP, 4 * HALF)))
    bias = jnp.concatenate(biases, axis=0)
    for b in range(HB):
        base = b * 2 * W_PAD
        head = slice(b * HD, (b + 1) * HD)
        key_w = jnp.concatenate([w_ref[j, base:base + W_PAD] for j in range(RING)], axis=0)
        value_w = jnp.concatenate([w_ref[j, base + W_PAD:base + 2 * W_PAD] for j in range(RING)], axis=0)
        weight = jnp.concatenate([key_w, value_w], axis=1)
        kv_own = jnp.dot(own, weight, preferred_element_type=jnp.float32).astype(jnp.bfloat16)
        kv_other = jnp.dot(other, weight, preferred_element_type=jnp.float32).astype(jnp.bfloat16)
        x = x_ref[:, head].astype(jnp.float32)
        q = (x * inv * gain_ref[:, head] * HD ** (-0.5)).astype(jnp.bfloat16)
        scores, values = [], []
        for c in range(groups):
            keys = slice(c * 2 * HALF, (c + 1) * 2 * HALF)
            key = jnp.concatenate([kv_own[keys, :HD], kv_other[keys, :HD]], axis=0)
            values.append(jnp.concatenate([kv_own[keys, HD:], kv_other[keys, HD:]], axis=0))
            scores.append(
                lax.dot_general(
                    q[c * GROUP:(c + 1) * GROUP],
                    key,
                    (((1,), (1,)), ((), ())),
                    preferred_element_type=jnp.float32,
                )
            )
        masked = jnp.concatenate(scores, axis=0) + bias
        row_max = jnp.max(masked, axis=1, keepdims=True)
        row_max = jnp.where(row_max > -1e29, row_max, 0.0)
        expo = jnp.exp(masked - row_max)
        total = jnp.maximum(jnp.sum(expo, axis=1, keepdims=True), 1.0)
        probs = (expo * (1.0 / total)).astype(jnp.bfloat16)
        attended = [
            jnp.dot(probs[c * GROUP:(c + 1) * GROUP], values[c], preferred_element_type=jnp.float32)
            for c in range(groups)
        ]
        out_ref[:, head] = (x + jnp.concatenate(attended, axis=0)).astype(jnp.bfloat16)


def attend(live, table, own, slabs, spread, weights, x, inv, gain):
    tokens, width = x.shape
    whole = lambda *shape: pl.BlockSpec(shape, lambda i, live, table: (0,) * len(shape))
    return pl.pallas_call(
        attend_kernel,
        grid_spec=pltpu.PrefetchScalarGridSpec(
            num_scalar_prefetch=2,
            grid=(HEADS_HERE // HB,),
            in_specs=[
                whole(REQ * HALF, ENC_PAD),
                whole(REQ, SLAB, HD),
                whole(2, ENC_PAD, ENC_PAD),
                pl.BlockSpec((RING, HB * 2 * W_PAD, HD), lambda i, live, table: (0, i, 0)),
                pl.BlockSpec((tokens, HB * HD), lambda i, live, table: (0, i)),
                whole(tokens, 1),
                pl.BlockSpec((1, HB * HD), lambda i, live, table: (0, i)),
            ],
            out_specs=pl.BlockSpec((tokens, HB * HD), lambda i, live, table: (0, i)),
            scratch_shapes=[pltpu.VMEM((REQ * HALF, ENC_PAD), jnp.bfloat16)],
        ),
        out_shape=jax.ShapeDtypeStruct((tokens, width), jnp.bfloat16),
        compiler_params=pltpu.CompilerParams(vmem_limit_bytes=58 * 2**20),
        name="attend_heads",
    )(live, table, own, slabs, spread, weights, x, inv, gain)


def ring_place(owner, core):
    x, y = owner // SIDE, owner % SIDE
    return jnp.where(core == 0, x, y), jnp.where(core == 0, y, x)


def spread_of(core, here):
    channel = lax.broadcasted_iota(jnp.int32, (ENC_PAD, ENC_PAD), 0)
    column = lax.broadcasted_iota(jnp.int32, (ENC_PAD, ENC_PAD), 1)

    def put(source):
        near, far = ring_place(source // W_PART, core)
        near = (near - ring_place(here, core)[0]) % SIDE
        place = (far * SIDE + near) * W_PAD + source % W_PART
        used = jnp.logical_and(source >= 0, source < ENC)
        return jnp.logical_and(used, place == column).astype(jnp.bfloat16)

    return jnp.stack([put(channel), put(channel - (ENC_PAD - ENC))])


def source_table(requests, core, here):
    owner, block = requests // 6, requests % 6
    near, far = ring_place(owner, core)
    far = (far - ring_place(here, core)[1]) % SIDE
    which = jnp.where(far < 2, far, jnp.where(far == 3, 4, jnp.where(near < 2, 2, 3)))
    chunk = jnp.where(which == 3, near - 2, near)
    odd = block % 2
    row = chunk * D_ROWS + (block // 2) * (TILES * HALF) + odd * (TILES - ENC_PAD // HD) * HALF
    return jnp.stack([which, row, odd])


def first_ring(piece):
    groups = ring_groups(lax.axis_size("segment"), 0)
    copies = jnp.tile(piece, (SIDE, 1))
    return lax.all_to_all(
        copies, ("segment", "db"), split_axis=0, concat_axis=0, tiled=True, axis_index_groups=groups
    )


def on_device(stream, gain, key_weight, value_weight, owners, blocks, valid, database):
    core = lax.axis_index("segment") % 2
    place = lax.axis_index("db")
    rows = stream[0]
    tokens, local_width = rows.shape
    full_width = local_width * lax.axis_size("mp")

    def pack_weight(w):
        return jnp.pad(w[0], ((0, W_PAD - W_PART), (0, 0)))

    packed_w = jnp.concatenate([pack_weight(key_weight), pack_weight(value_weight)], axis=0)
    packed_w = packed_w.reshape(2 * W_PAD, HEADS_HERE, HD).transpose(1, 0, 2).reshape(W_ROWS, HD)

    half = lax.dynamic_slice(database, (0, core * HALF, 0), (2 * PAIRS, HALF, ENC))
    paired = jnp.concatenate([half[0::2], half[1::2]], axis=2)
    packed_d = paired.reshape(PAIRS, HALF, TILES, HD).transpose(0, 2, 1, 3).reshape(D_ROWS, HD)

    as_float = rows.astype(jnp.float32)
    squares = jnp.sum(as_float * as_float, axis=1)
    requests = (owners[0] * 6 + blocks[0]).reshape(-1)
    info = jnp.concatenate(
        [squares, gain[0], valid[0].reshape(-1).astype(jnp.float32), requests.astype(jnp.float32)]
    )
    info = jnp.pad(info, (0, -info.shape[0] % 1024)).reshape(-1, HD)
    info_here = to_next(info).reshape(-1)
    requests_other = to_next_other_core(requests)
    x_here = to_next(rows)

    line_d = first_ring(packed_d)
    pieces_w = [to_next_turned(packed_w, turn) for turn in (0, -1, 2, 1)]
    spread = spread_of(core, place)
    pieces_w, line_d, info_here, requests_other, spread = lax.optimization_barrier(
        (pieces_w, line_d, info_here, requests_other, spread)
    )
    all_w = lax.all_gather(
        jnp.concatenate(pieces_w, axis=0),
        ("segment", "db"),
        axis=0,
        tiled=True,
        axis_index_groups=ring_groups(lax.axis_size("segment"), 1),
    ).reshape(RING, W_ROWS, HD)
    d_before, d_after = turned(line_d, 1, 1), turned(line_d, -1, 1)
    mid_d = line_d.shape[0] // 2
    d_pieces = (line_d, d_after, turned(d_before[:mid_d], 1, 1), turned(d_after[mid_d:], -1, 1), d_before)

    squares_here = info_here[:tokens]
    squares_other = other_mp(squares_here.reshape(-1, HD)).reshape(-1)
    gain_here = info_here[tokens:tokens + local_width]
    ints = info_here[tokens + local_width:tokens + local_width + 2 * REQ].astype(jnp.int32)
    live, requests_here = ints[:REQ], ints[REQ:]
    table = jnp.concatenate(
        [source_table(requests_here, core, place), source_table(requests_other, core, place)], axis=1
    )

    given, squares_other, x_here = lax.optimization_barrier((give(table, d_pieces), squares_other, x_here))
    slabs = other_core(given)
    own = pick(table, d_pieces, spread)
    inv_rms = lax.rsqrt((squares_here + squares_other) / full_width + eps_norm)
    updated = attend(live, table, own, slabs, spread, all_w, x_here, inv_rms[:, None], gain_here[None, :])
    return updated[None]


def solution(mesh):
    return jax.shard_map(
        on_device,
        mesh=mesh,
        in_specs=(
            P("segment", "db", "mp"),
            P("segment", "mp"),
            P("segment", "db", "mp"),
            P("segment", "db", "mp"),
            P("segment", "db", None),
            P("segment", "db", None),
            P("segment", "db", None),
            P("db", None, None),
        ),
        out_specs=P("segment", "db", "mp"),
        check_vma=False,
    )
```

```python
import jax
import jax.numpy as jnp
from jax import lax
from jax.experimental import pallas as pl
from jax.experimental.pallas import tpu as pltpu
from jax.sharding import PartitionSpec as P

HD = 128
GROUP = 64
SIDE = 4
RING = SIDE * SIDE
eps_norm = 1e-06

W_PART = 28
W_PAD = 32
HEADS_HERE = 16
W_ROWS = HEADS_HERE * 2 * W_PAD
ENC = 448
ENC_PAD = RING * W_PAD
SHIFT = ENC_PAD - ENC
HALF = 64
TILES = 2 * ENC // HD
PAIRS = 3
D_ROWS = PAIRS * TILES * HALF
SLAB = ENC_PAD // HD * HALF
REQ = 12
HB = 4


def ring_pairs(segments, turn, along_x_core):
    pairs = []
    for seg in range(segments):
        for place in range(RING):
            x, y = divmod(place, SIDE)
            if seg % 2 == along_x_core:
                to = ((x + turn) % SIDE) * SIDE + y
            else:
                to = x * SIDE + (y + turn) % SIDE
            pairs.append((seg * RING + place, seg * RING + to))
    return pairs


def ring_groups(segments, along_x_core):
    groups = []
    for seg in range(segments):
        for line in range(SIDE):
            if seg % 2 == along_x_core:
                groups.append([seg * RING + x * SIDE + line for x in range(SIDE)])
            else:
                groups.append([seg * RING + line * SIDE + y for y in range(SIDE)])
    return groups


def turned(value, turn, along_x_core):
    pairs = ring_pairs(lax.axis_size("segment"), turn, along_x_core)
    return lax.ppermute(value, ("segment", "db"), pairs)


def to_next_turned(value, turn):
    count = lax.axis_size("segment")
    behind = ring_pairs(count, turn, 0)
    pairs = [(((seg - 1) % count) * RING + place, to) for seg in range(count) for place, to in
             [(source % RING, target) for source, target in behind[seg * RING:(seg + 1) * RING]]]
    return lax.ppermute(value, ("segment", "db"), pairs)


def to_next(value):
    count = lax.axis_size("segment")
    return lax.ppermute(value, "segment", [(s, (s + 1) % count) for s in range(count)])


def to_next_other_core(value):
    count = lax.axis_size("segment")
    return lax.ppermute(value, "segment", [(s, ((s + 1) % count) ^ 1) for s in range(count)])


def other_mp(value):
    return lax.ppermute(value, "mp", [(0, 1), (1, 0)])


def other_core(value):
    count = lax.axis_size("segment")
    return lax.ppermute(value, "segment", [(s, s ^ 1) for s in range(count)])


def fetch(table, first, sources, slabs, sems):
    def begin(i, carry):
        which = table[0, first + i]
        row = pl.multiple_of(table[1, first + i], 64)
        for number, source in enumerate(sources):
            @pl.when(which == number)
            def _():
                pltpu.make_async_copy(source.at[pl.ds(row, SLAB)], slabs.at[i], sems.at[i]).start()
        return carry

    def finish(i, carry):
        pltpu.make_async_copy(sources[0].at[pl.ds(0, SLAB)], slabs.at[i], sems.at[i]).wait()
        return carry

    lax.fori_loop(0, REQ, begin, 0)
    lax.fori_loop(0, REQ, finish, 0)


def spread_slabs(table, slabs, spread):
    tiles = ENC_PAD // HD
    rows = []
    for i in range(REQ):
        slab = slabs[i]
        rows.append(jnp.concatenate([slab[t * HALF:(t + 1) * HALF] for t in range(tiles)], axis=1))
    stacked = jnp.concatenate(rows, axis=0)
    even = jnp.dot(stacked, spread[SHIFT:], preferred_element_type=jnp.float32)
    odd = jnp.dot(stacked, spread[:ENC_PAD], preferred_element_type=jnp.float32)
    placed = []
    for i in range(REQ):
        here = slice(i * HALF, (i + 1) * HALF)
        placed.append(jnp.where(table[2, i] == 1, odd[here], even[here]).astype(jnp.bfloat16))
    return placed


def give_kernel(table, c_ref, r_ref, ol_ref, or_ref, l_ref, out_ref, sems):
    fetch(table, REQ, (c_ref, r_ref, ol_ref, or_ref, l_ref), out_ref, sems)


def pick_kernel(table, c_ref, r_ref, ol_ref, or_ref, l_ref, spread, out_ref, slabs, sems):
    fetch(table, 0, (c_ref, r_ref, ol_ref, or_ref, l_ref), slabs, sems)
    for i, block in enumerate(spread_slabs(table, slabs, spread)):
        out_ref[i * HALF:(i + 1) * HALF] = block


SMEM = pl.BlockSpec(memory_space=pltpu.SMEM)
VMEM = pl.BlockSpec(memory_space=pltpu.VMEM)
ANY = pl.BlockSpec(memory_space=pl.ANY)


def give(table, pieces):
    return pl.pallas_call(
        give_kernel,
        in_specs=[SMEM] + [ANY] * 5,
        out_specs=VMEM,
        out_shape=jax.ShapeDtypeStruct((REQ, SLAB, HD), jnp.bfloat16),
        scratch_shapes=[pltpu.SemaphoreType.DMA((REQ,))],
        compiler_params=pltpu.CompilerParams(vmem_limit_bytes=16 * 2**20),
        name="give_encodings",
    )(table, *pieces)


def pick(table, pieces, spread):
    return pl.pallas_call(
        pick_kernel,
        in_specs=[SMEM] + [ANY] * 5 + [VMEM],
        out_specs=VMEM,
        out_shape=jax.ShapeDtypeStruct((REQ * HALF, ENC_PAD), jnp.bfloat16),
        scratch_shapes=[
            pltpu.VMEM((REQ, SLAB, HD), jnp.bfloat16),
            pltpu.SemaphoreType.DMA((REQ,)),
        ],
        compiler_params=pltpu.CompilerParams(vmem_limit_bytes=32 * 2**20),
        name="pick_encodings",
    )(table, *pieces, spread)


def attend_kernel(
    live, table, own_ref, slabs, spread, w_ref, x_ref, inv_ref, gain_ref, out_ref, other_ref
):

    @pl.when(pl.program_id(0) == 0)
    def _():
        for i, block in enumerate(spread_slabs(table, slabs, spread)):
            other_ref[i * HALF:(i + 1) * HALF] = block

    own, other = own_ref[...], other_ref[...]
    inv = inv_ref[...]
    groups = x_ref.shape[0] // GROUP
    column = lax.broadcasted_iota(jnp.int32, (1, HD), 1)
    biases = []
    for c in range(groups):
        bias = jnp.where(jnp.where(column < HALF, live[2 * c], live[2 * c + 1]) > 0, 0.0, -1e30)
        biases.append(jnp.broadcast_to(jnp.concatenate([bias, bias], axis=1), (GROUP, 4 * HALF)))
    bias = jnp.concatenate(biases, axis=0)
    for b in range(HB):
        base = b * 2 * W_PAD
        head = slice(b * HD, (b + 1) * HD)
        key_w = jnp.concatenate([w_ref[j, base:base + W_PAD] for j in range(RING)], axis=0)
        value_w = jnp.concatenate([w_ref[j, base + W_PAD:base + 2 * W_PAD] for j in range(RING)], axis=0)
        weight = jnp.concatenate([key_w, value_w], axis=1)
        kv_own = jnp.dot(own, weight, preferred_element_type=jnp.float32).astype(jnp.bfloat16)
        kv_other = jnp.dot(other, weight, preferred_element_type=jnp.float32).astype(jnp.bfloat16)
        x = x_ref[:, head].astype(jnp.float32)
        q = (x * inv * gain_ref[:, head] * HD ** (-0.5)).astype(jnp.bfloat16)
        scores, values = [], []
        for c in range(groups):
            keys = slice(c * 2 * HALF, (c + 1) * 2 * HALF)
            key = jnp.concatenate([kv_own[keys, :HD], kv_other[keys, :HD]], axis=0)
            values.append(jnp.concatenate([kv_own[keys, HD:], kv_other[keys, HD:]], axis=0))
            scores.append(
                lax.dot_general(
                    q[c * GROUP:(c + 1) * GROUP],
                    key,
                    (((1,), (1,)), ((), ())),
                    preferred_element_type=jnp.float32,
                )
            )
        masked = jnp.concatenate(scores, axis=0) + bias
        row_max = jnp.max(masked, axis=1, keepdims=True)
        row_max = jnp.where(row_max > -1e29, row_max, 0.0)
        expo = jnp.exp(masked - row_max)
        total = jnp.maximum(jnp.sum(expo, axis=1, keepdims=True), 1.0)
        probs = (expo * (1.0 / total)).astype(jnp.bfloat16)
        attended = [
            jnp.dot(probs[c * GROUP:(c + 1) * GROUP], values[c], preferred_element_type=jnp.float32)
            for c in range(groups)
        ]
        out_ref[:, head] = (x + jnp.concatenate(attended, axis=0)).astype(jnp.bfloat16)


def attend(live, table, own, slabs, spread, weights, x, inv, gain):
    tokens, width = x.shape
    whole = lambda *shape: pl.BlockSpec(shape, lambda i, live, table: (0,) * len(shape))
    return pl.pallas_call(
        attend_kernel,
        grid_spec=pltpu.PrefetchScalarGridSpec(
            num_scalar_prefetch=2,
            grid=(HEADS_HERE // HB,),
            in_specs=[
                whole(REQ * HALF, ENC_PAD),
                whole(REQ, SLAB, HD),
                whole(SHIFT + ENC_PAD, ENC_PAD),
                pl.BlockSpec((RING, HB * 2 * W_PAD, HD), lambda i, live, table: (0, i, 0)),
                pl.BlockSpec((tokens, HB * HD), lambda i, live, table: (0, i)),
                whole(tokens, 1),
                pl.BlockSpec((1, HB * HD), lambda i, live, table: (0, i)),
            ],
            out_specs=pl.BlockSpec((tokens, HB * HD), lambda i, live, table: (0, i)),
            scratch_shapes=[pltpu.VMEM((REQ * HALF, ENC_PAD), jnp.bfloat16)],
        ),
        out_shape=jax.ShapeDtypeStruct((tokens, width), jnp.bfloat16),
        compiler_params=pltpu.CompilerParams(vmem_limit_bytes=58 * 2**20),
        name="attend_heads",
    )(live, table, own, slabs, spread, weights, x, inv, gain)


def ring_place(owner, core):
    x, y = owner // SIDE, owner % SIDE
    return jnp.where(core == 0, x, y), jnp.where(core == 0, y, x)


def spread_of(core, here):
    channel = jnp.arange(SHIFT + ENC_PAD) - SHIFT
    near, far = ring_place(channel // W_PART, core)
    near = (near - ring_place(here, core)[0]) % SIDE
    place = (far * SIDE + near) * W_PAD + channel % W_PART
    used = jnp.logical_and(channel >= 0, channel < ENC)
    place = lax.optimization_barrier(jnp.where(used, place, -1))
    column = lax.broadcasted_iota(jnp.int32, (SHIFT + ENC_PAD, ENC_PAD), 1)
    return (place[:, None] == column).astype(jnp.bfloat16)


def source_table(requests, core, here):
    owner, block = requests // 6, requests % 6
    near, far = ring_place(owner, core)
    near_here, far_here = ring_place(here, core)
    near, far = (near - near_here) % SIDE, (far - far_here) % SIDE
    which = jnp.where(far < 2, far, jnp.where(far == 3, 4, jnp.where(near < 2, 2, 3)))
    chunk = jnp.where(which == 3, near - 2, near)
    odd = block % 2
    row = chunk * D_ROWS + (block // 2) * (TILES * HALF) + odd * (TILES - ENC_PAD // HD) * HALF
    return jnp.stack([which, row, odd])


def in_three(value):
    parts = []
    for _ in range(3):
        part = lax.reduce_precision(value, 8, 7)
        parts.append(part.astype(jnp.bfloat16))
        value = value - part
    return jnp.stack(parts)


def from_three(parts):
    high, mid, low = parts.astype(jnp.float32)
    return high + (mid + low)


def on_device(stream, gain, key_weight, value_weight, owners, blocks, valid, database):
    core = lax.axis_index("segment") % 2
    place = lax.axis_index("db")
    rows = stream[0]
    tokens, local_width = rows.shape
    full_width = local_width * lax.axis_size("mp")

    def pack_weight(w):
        return jnp.pad(w[0], ((0, W_PAD - W_PART), (0, 0)))

    packed_w = jnp.concatenate([pack_weight(key_weight), pack_weight(value_weight)], axis=0)
    packed_w = packed_w.reshape(2 * W_PAD, HEADS_HERE, HD).transpose(1, 0, 2).reshape(W_ROWS, HD)

    half = lax.dynamic_slice(database, (0, core * HALF, 0), (2 * PAIRS, HALF, ENC))
    paired = jnp.concatenate([half[0::2], half[1::2]], axis=2)
    packed_d = paired.reshape(PAIRS, HALF, TILES, HD).transpose(0, 2, 1, 3).reshape(D_ROWS, HD)

    as_float = rows.astype(jnp.float32)
    squares = jnp.sum(as_float * as_float, axis=1)
    requests = (owners[0] * 6 + blocks[0]).reshape(-1)
    info = jnp.concatenate(
        [squares, gain[0], valid[0].reshape(-1).astype(jnp.float32), requests.astype(jnp.float32)]
    )
    info_rows = -(-info.shape[0] // HD)
    info = jnp.pad(info, (0, info_rows * HD - info.shape[0]))
    sent = in_three(info).reshape(3 * info_rows, HD)
    sent = jnp.pad(sent, ((0, -sent.shape[0] % 16), (0, 0)))
    requests_other = to_next_other_core(requests)
    x_here = to_next(rows)

    pieces_d = [packed_d] + [turned(packed_d, turn, 0) for turn in (-1, 2, 1)]
    line_d = jnp.concatenate(pieces_d, axis=0)
    next_w = to_next_turned(jnp.concatenate([packed_w, sent], axis=0), 0)
    pieces_w = [next_w[:W_ROWS]] + [to_next_turned(packed_w, turn) for turn in (-1, 2, 1)]
    all_w = lax.all_gather(
        jnp.concatenate(pieces_w, axis=0),
        ("segment", "db"),
        axis=0,
        tiled=True,
        axis_index_groups=ring_groups(lax.axis_size("segment"), 1),
    ).reshape(RING, W_ROWS, HD)
    d_before, d_after = turned(line_d, 1, 1), turned(line_d, -1, 1)
    info_here = from_three(next_w[W_ROWS:W_ROWS + 3 * info_rows].reshape(3, info_rows * HD))
    spread = spread_of(core, place)
    d_before, d_after, spread, requests_other = lax.optimization_barrier((d_before, d_after, spread, requests_other))
    mid_d = line_d.shape[0] // 2
    d_pieces = (line_d, d_after, turned(d_before[:mid_d], 1, 1), turned(d_after[mid_d:], -1, 1), d_before)

    squares_here = info_here[:tokens]
    squares_other = other_mp(squares_here.reshape(-1, HD)).reshape(-1)
    gain_here = info_here[tokens:tokens + local_width]
    ints = info_here[tokens + local_width:tokens + local_width + 2 * REQ].astype(jnp.int32)
    live, requests_here = ints[:REQ], ints[REQ:]
    table = jnp.concatenate(
        [source_table(requests_here, core, place), source_table(requests_other, core, place)], axis=1
    )

    given, squares_other, x_here = lax.optimization_barrier((give(table, d_pieces), squares_other, x_here))
    slabs = other_core(given)
    own = pick(table, d_pieces, spread)
    inv_rms = lax.rsqrt((squares_here + squares_other) / full_width + eps_norm)
    updated = attend(live, table, own, slabs, spread, all_w, x_here, inv_rms[:, None], gain_here[None, :])
    return updated[None]


def solution(mesh):
    return jax.shard_map(
        on_device,
        mesh=mesh,
        in_specs=(
            P("segment", "db", "mp"),
            P("segment", "mp"),
            P("segment", "db", "mp"),
            P("segment", "db", "mp"),
            P("segment", "db", None),
            P("segment", "db", None),
            P("segment", "db", None),
            P("db", None, None),
        ),
        out_specs=P("segment", "db", "mp"),
        check_vma=False,
    )
```

```python
import jax
import jax.numpy as jnp
from jax import lax
from jax.experimental import pallas as pl
from jax.experimental.pallas import tpu as pltpu
from jax.sharding import PartitionSpec as P

HD = 128
GROUP = 64
SIDE = 4
RING = SIDE * SIDE
eps_norm = 1e-06

W_PART = 28
W_PAD = 32
HEADS_HERE = 16
W_ROWS = HEADS_HERE * 2 * W_PAD
ENC = 448
ENC_PAD = RING * W_PAD
SHIFT = ENC_PAD - ENC
HALF = 64
TILES = 2 * ENC // HD
PAIRS = 3
D_ROWS = PAIRS * TILES * HALF
SLAB = ENC_PAD // HD * HALF
REQ = 12
HB = 4


def ring_pairs(segments, turn, along_x_core):
    pairs = []
    for seg in range(segments):
        for place in range(RING):
            x, y = divmod(place, SIDE)
            if seg % 2 == along_x_core:
                to = ((x + turn) % SIDE) * SIDE + y
            else:
                to = x * SIDE + (y + turn) % SIDE
            pairs.append((seg * RING + place, seg * RING + to))
    return pairs


def ring_groups(segments, along_x_core):
    groups = []
    for seg in range(segments):
        for line in range(SIDE):
            if seg % 2 == along_x_core:
                groups.append([seg * RING + x * SIDE + line for x in range(SIDE)])
            else:
                groups.append([seg * RING + line * SIDE + y for y in range(SIDE)])
    return groups


def turned(value, turn, along_x_core):
    pairs = ring_pairs(lax.axis_size("segment"), turn, along_x_core)
    return lax.ppermute(value, ("segment", "db"), pairs)


def to_next_turned(value, turn):
    count = lax.axis_size("segment")
    behind = ring_pairs(count, turn, 0)
    pairs = [(((seg - 1) % count) * RING + place, to) for seg in range(count) for place, to in
             [(source % RING, target) for source, target in behind[seg * RING:(seg + 1) * RING]]]
    return lax.ppermute(value, ("segment", "db"), pairs)


def to_next(value):
    count = lax.axis_size("segment")
    return lax.ppermute(value, "segment", [(s, (s + 1) % count) for s in range(count)])


def to_next_other_core(value):
    count = lax.axis_size("segment")
    return lax.ppermute(value, "segment", [(s, ((s + 1) % count) ^ 1) for s in range(count)])


def other_mp(value):
    return lax.ppermute(value, "mp", [(0, 1), (1, 0)])


def other_core(value):
    count = lax.axis_size("segment")
    return lax.ppermute(value, "segment", [(s, s ^ 1) for s in range(count)])


def fetch(table, first, sources, slabs, sems):
    def begin(i, carry):
        which = table[0, first + i]
        row = pl.multiple_of(table[1, first + i], 64)
        for number, source in enumerate(sources):
            @pl.when(which == number)
            def _():
                pltpu.make_async_copy(source.at[pl.ds(row, SLAB)], slabs.at[i], sems.at[i]).start()
        return carry

    def finish(i, carry):
        pltpu.make_async_copy(sources[0].at[pl.ds(0, SLAB)], slabs.at[i], sems.at[i]).wait()
        return carry

    lax.fori_loop(0, REQ, begin, 0)
    lax.fori_loop(0, REQ, finish, 0)


def spread_slabs(table, slabs, spread):
    tiles = ENC_PAD // HD
    rows = []
    for i in range(REQ):
        slab = slabs[i]
        rows.append(jnp.concatenate([slab[t * HALF:(t + 1) * HALF] for t in range(tiles)], axis=1))
    stacked = jnp.concatenate(rows, axis=0)
    even = jnp.dot(stacked, spread[SHIFT:], preferred_element_type=jnp.float32)
    odd = jnp.dot(stacked, spread[:ENC_PAD], preferred_element_type=jnp.float32)
    placed = []
    for i in range(REQ):
        here = slice(i * HALF, (i + 1) * HALF)
        placed.append(jnp.where(table[2, i] == 1, odd[here], even[here]).astype(jnp.bfloat16))
    return placed


def give_kernel(table, c_ref, r_ref, ol_ref, or_ref, l_ref, out_ref, sems):
    fetch(table, REQ, (c_ref, r_ref, ol_ref, or_ref, l_ref), out_ref, sems)


def pick_kernel(table, c_ref, r_ref, ol_ref, or_ref, l_ref, spread, out_ref, slabs, sems):
    fetch(table, 0, (c_ref, r_ref, ol_ref, or_ref, l_ref), slabs, sems)
    for i, block in enumerate(spread_slabs(table, slabs, spread)):
        out_ref[i * HALF:(i + 1) * HALF] = block


SMEM = pl.BlockSpec(memory_space=pltpu.SMEM)
VMEM = pl.BlockSpec(memory_space=pltpu.VMEM)
ANY = pl.BlockSpec(memory_space=pl.ANY)


def give(table, pieces):
    return pl.pallas_call(
        give_kernel,
        in_specs=[SMEM] + [ANY] * 5,
        out_specs=VMEM,
        out_shape=jax.ShapeDtypeStruct((REQ, SLAB, HD), jnp.bfloat16),
        scratch_shapes=[pltpu.SemaphoreType.DMA((REQ,))],
        compiler_params=pltpu.CompilerParams(vmem_limit_bytes=16 * 2**20),
        name="give_encodings",
    )(table, *pieces)


def pick(table, pieces, spread):
    return pl.pallas_call(
        pick_kernel,
        in_specs=[SMEM] + [ANY] * 5 + [VMEM],
        out_specs=VMEM,
        out_shape=jax.ShapeDtypeStruct((REQ * HALF, ENC_PAD), jnp.bfloat16),
        scratch_shapes=[
            pltpu.VMEM((REQ, SLAB, HD), jnp.bfloat16),
            pltpu.SemaphoreType.DMA((REQ,)),
        ],
        compiler_params=pltpu.CompilerParams(vmem_limit_bytes=32 * 2**20),
        name="pick_encodings",
    )(table, *pieces, spread)


def attend_kernel(
    live, table, own_ref, slabs, spread, w_ref, x_ref, inv_ref, gain_ref, out_ref, other_ref
):

    @pl.when(pl.program_id(0) == 0)
    def _():
        for i, block in enumerate(spread_slabs(table, slabs, spread)):
            other_ref[i * HALF:(i + 1) * HALF] = block

    own, other = own_ref[...], other_ref[...]
    inv = inv_ref[...]
    groups = x_ref.shape[0] // GROUP
    column = lax.broadcasted_iota(jnp.int32, (1, HD), 1)
    biases = []
    for c in range(groups):
        bias = jnp.where(jnp.where(column < HALF, live[2 * c], live[2 * c + 1]) > 0, 0.0, -1e30)
        biases.append(jnp.broadcast_to(jnp.concatenate([bias, bias], axis=1), (GROUP, 4 * HALF)))
    bias = jnp.concatenate(biases, axis=0)
    for b in range(HB):
        base = b * 2 * W_PAD
        head = slice(b * HD, (b + 1) * HD)
        key_w = jnp.concatenate([w_ref[j, base:base + W_PAD] for j in range(RING)], axis=0)
        value_w = jnp.concatenate([w_ref[j, base + W_PAD:base + 2 * W_PAD] for j in range(RING)], axis=0)
        weight = jnp.concatenate([key_w, value_w], axis=1)
        kv_own = jnp.dot(own, weight, preferred_element_type=jnp.float32).astype(jnp.bfloat16)
        kv_other = jnp.dot(other, weight, preferred_element_type=jnp.float32).astype(jnp.bfloat16)
        x = x_ref[:, head].astype(jnp.float32)
        q = (x * inv * gain_ref[:, head] * HD ** (-0.5)).astype(jnp.bfloat16)
        scores, values = [], []
        for c in range(groups):
            keys = slice(c * 2 * HALF, (c + 1) * 2 * HALF)
            key = jnp.concatenate([kv_own[keys, :HD], kv_other[keys, :HD]], axis=0)
            values.append(jnp.concatenate([kv_own[keys, HD:], kv_other[keys, HD:]], axis=0))
            scores.append(
                lax.dot_general(
                    q[c * GROUP:(c + 1) * GROUP],
                    key,
                    (((1,), (1,)), ((), ())),
                    preferred_element_type=jnp.float32,
                )
            )
        masked = jnp.concatenate(scores, axis=0) + bias
        row_max = jnp.max(masked, axis=1, keepdims=True)
        row_max = jnp.where(row_max > -1e29, row_max, 0.0)
        expo = jnp.exp(masked - row_max)
        total = jnp.maximum(jnp.sum(expo, axis=1, keepdims=True), 1.0)
        probs = (expo * (1.0 / total)).astype(jnp.bfloat16)
        attended = [
            jnp.dot(probs[c * GROUP:(c + 1) * GROUP], values[c], preferred_element_type=jnp.float32)
            for c in range(groups)
        ]
        out_ref[:, head] = (x + jnp.concatenate(attended, axis=0)).astype(jnp.bfloat16)


def attend(live, table, own, slabs, spread, weights, x, inv, gain):
    tokens, width = x.shape
    whole = lambda *shape: pl.BlockSpec(shape, lambda i, live, table: (0,) * len(shape))
    return pl.pallas_call(
        attend_kernel,
        grid_spec=pltpu.PrefetchScalarGridSpec(
            num_scalar_prefetch=2,
            grid=(HEADS_HERE // HB,),
            in_specs=[
                whole(REQ * HALF, ENC_PAD),
                whole(REQ, SLAB, HD),
                whole(SHIFT + ENC_PAD, ENC_PAD),
                pl.BlockSpec((RING, HB * 2 * W_PAD, HD), lambda i, live, table: (0, i, 0)),
                pl.BlockSpec((tokens, HB * HD), lambda i, live, table: (0, i)),
                whole(tokens, 1),
                pl.BlockSpec((1, HB * HD), lambda i, live, table: (0, i)),
            ],
            out_specs=pl.BlockSpec((tokens, HB * HD), lambda i, live, table: (0, i)),
            scratch_shapes=[pltpu.VMEM((REQ * HALF, ENC_PAD), jnp.bfloat16)],
        ),
        out_shape=jax.ShapeDtypeStruct((tokens, width), jnp.bfloat16),
        compiler_params=pltpu.CompilerParams(vmem_limit_bytes=58 * 2**20),
        name="attend_heads",
    )(live, table, own, slabs, spread, weights, x, inv, gain)


def ring_place(owner, core):
    x, y = owner // SIDE, owner % SIDE
    return jnp.where(core == 0, x, y), jnp.where(core == 0, y, x)


def spread_of(core, here):
    channel = jnp.arange(SHIFT + ENC_PAD) - SHIFT
    near, far = ring_place(channel // W_PART, core)
    near = (near - ring_place(here, core)[0]) % SIDE
    place = (far * SIDE + near) * W_PAD + channel % W_PART
    used = jnp.logical_and(channel >= 0, channel < ENC)
    place = lax.optimization_barrier(jnp.where(used, place, -1))
    column = lax.broadcasted_iota(jnp.int32, (SHIFT + ENC_PAD, ENC_PAD), 1)
    return (place[:, None] == column).astype(jnp.bfloat16)


def source_table(requests, core, here):
    owner, block = requests // 6, requests % 6
    near, far = ring_place(owner, core)
    far = (far - ring_place(here, core)[1]) % SIDE
    which = jnp.where(far < 2, far, jnp.where(far == 3, 4, jnp.where(near < 2, 2, 3)))
    chunk = jnp.where(which == 3, near - 2, near)
    odd = block % 2
    row = chunk * D_ROWS + (block // 2) * (TILES * HALF) + odd * (TILES - ENC_PAD // HD) * HALF
    return jnp.stack([which, row, odd])


def first_ring(piece):
    groups = ring_groups(lax.axis_size("segment"), 0)
    copies = jnp.tile(piece, (SIDE, 1))
    return lax.all_to_all(
        copies, ("segment", "db"), split_axis=0, concat_axis=0, tiled=True, axis_index_groups=groups
    )


def on_device(stream, gain, key_weight, value_weight, owners, blocks, valid, database):
    core = lax.axis_index("segment") % 2
    place = lax.axis_index("db")
    rows = stream[0]
    tokens, local_width = rows.shape
    full_width = local_width * lax.axis_size("mp")

    def pack_weight(w):
        return jnp.pad(w[0], ((0, W_PAD - W_PART), (0, 0)))

    packed_w = jnp.concatenate([pack_weight(key_weight), pack_weight(value_weight)], axis=0)
    packed_w = packed_w.reshape(2 * W_PAD, HEADS_HERE, HD).transpose(1, 0, 2).reshape(W_ROWS, HD)

    half = lax.dynamic_slice(database, (0, core * HALF, 0), (2 * PAIRS, HALF, ENC))
    paired = jnp.concatenate([half[0::2], half[1::2]], axis=2)
    packed_d = paired.reshape(PAIRS, HALF, TILES, HD).transpose(0, 2, 1, 3).reshape(D_ROWS, HD)

    as_float = rows.astype(jnp.float32)
    squares = jnp.sum(as_float * as_float, axis=1)
    requests = (owners[0] * 6 + blocks[0]).reshape(-1)
    info = jnp.concatenate(
        [squares, gain[0], valid[0].reshape(-1).astype(jnp.float32), requests.astype(jnp.float32)]
    )
    info = jnp.pad(info, (0, -info.shape[0] % 1024)).reshape(-1, HD)

    pieces_w = [to_next_turned(packed_w, turn) for turn in (0, -1, 2, 1)]
    pieces_w, line_d, info, requests, rows = lax.optimization_barrier(
        (pieces_w, first_ring(packed_d), info, requests, rows)
    )
    all_w = lax.all_gather(
        jnp.concatenate(pieces_w, axis=0),
        ("segment", "db"),
        axis=0,
        tiled=True,
        axis_index_groups=ring_groups(lax.axis_size("segment"), 1),
    ).reshape(RING, W_ROWS, HD)
    d_before, d_after = turned(line_d, 1, 1), turned(line_d, -1, 1)
    info_here = to_next(info).reshape(-1)
    requests_other = to_next_other_core(requests)
    x_here = to_next(rows)
    spread = spread_of(core, place)
    d_before, d_after, spread, requests_other = lax.optimization_barrier((d_before, d_after, spread, requests_other))
    mid_d = line_d.shape[0] // 2
    d_pieces = (line_d, d_after, turned(d_before[:mid_d], 1, 1), turned(d_after[mid_d:], -1, 1), d_before)

    squares_here = info_here[:tokens]
    squares_other = other_mp(squares_here.reshape(-1, HD)).reshape(-1)
    gain_here = info_here[tokens:tokens + local_width]
    ints = info_here[tokens + local_width:tokens + local_width + 2 * REQ].astype(jnp.int32)
    live, requests_here = ints[:REQ], ints[REQ:]
    table = jnp.concatenate(
        [source_table(requests_here, core, place), source_table(requests_other, core, place)], axis=1
    )

    given, squares_other, x_here = lax.optimization_barrier((give(table, d_pieces), squares_other, x_here))
    slabs = other_core(given)
    own = pick(table, d_pieces, spread)
    inv_rms = lax.rsqrt((squares_here + squares_other) / full_width + eps_norm)
    updated = attend(live, table, own, slabs, spread, all_w, x_here, inv_rms[:, None], gain_here[None, :])
    return updated[None]


def solution(mesh):
    return jax.shard_map(
        on_device,
        mesh=mesh,
        in_specs=(
            P("segment", "db", "mp"),
            P("segment", "mp"),
            P("segment", "db", "mp"),
            P("segment", "db", "mp"),
            P("segment", "db", None),
            P("segment", "db", None),
            P("segment", "db", None),
            P("db", None, None),
        ),
        out_specs=P("segment", "db", "mp"),
        check_vma=False,
    )
```

```python
import jax
import jax.numpy as jnp
from jax import lax
from jax.experimental import pallas as pl
from jax.experimental.pallas import tpu as pltpu
from jax.sharding import PartitionSpec as P

HD = 128
GROUP = 64
SIDE = 4
RING = SIDE * SIDE
eps_norm = 1e-06

W_PART = 28
W_PAD = 32
HEADS_HERE = 16
W_ROWS = HEADS_HERE * 2 * W_PAD
ENC = 448
ENC_PAD = RING * W_PAD
SHIFT = ENC_PAD - ENC
HALF = 64
TILES = 2 * ENC // HD
PAIRS = 3
D_ROWS = PAIRS * TILES * HALF
SLAB = ENC_PAD // HD * HALF
REQ = 12
HB = 4


def ring_pairs(segments, turn, along_x_core):
    pairs = []
    for seg in range(segments):
        for place in range(RING):
            x, y = divmod(place, SIDE)
            if seg % 2 == along_x_core:
                to = ((x + turn) % SIDE) * SIDE + y
            else:
                to = x * SIDE + (y + turn) % SIDE
            pairs.append((seg * RING + place, seg * RING + to))
    return pairs


def ring_groups(segments, along_x_core):
    groups = []
    for seg in range(segments):
        for line in range(SIDE):
            if seg % 2 == along_x_core:
                groups.append([seg * RING + x * SIDE + line for x in range(SIDE)])
            else:
                groups.append([seg * RING + line * SIDE + y for y in range(SIDE)])
    return groups


def turned(value, turn, along_x_core):
    pairs = ring_pairs(lax.axis_size("segment"), turn, along_x_core)
    return lax.ppermute(value, ("segment", "db"), pairs)


def to_next_turned(value, turn):
    count = lax.axis_size("segment")
    behind = ring_pairs(count, turn, 0)
    pairs = [(((seg - 1) % count) * RING + place, to) for seg in range(count) for place, to in
             [(source % RING, target) for source, target in behind[seg * RING:(seg + 1) * RING]]]
    return lax.ppermute(value, ("segment", "db"), pairs)


def to_next(value):
    count = lax.axis_size("segment")
    return lax.ppermute(value, "segment", [(s, (s + 1) % count) for s in range(count)])


def to_next_other_core(value):
    count = lax.axis_size("segment")
    return lax.ppermute(value, "segment", [(s, ((s + 1) % count) ^ 1) for s in range(count)])


def other_mp(value):
    return lax.ppermute(value, "mp", [(0, 1), (1, 0)])


def other_core(value):
    count = lax.axis_size("segment")
    return lax.ppermute(value, "segment", [(s, s ^ 1) for s in range(count)])


def fetch(table, first, sources, slabs, sems):
    def begin(i, carry):
        which = table[0, first + i]
        row = pl.multiple_of(table[1, first + i], 64)
        for number, source in enumerate(sources):
            @pl.when(which == number)
            def _():
                pltpu.make_async_copy(source.at[pl.ds(row, SLAB)], slabs.at[i], sems.at[i]).start()
        return carry

    def finish(i, carry):
        pltpu.make_async_copy(sources[0].at[pl.ds(0, SLAB)], slabs.at[i], sems.at[i]).wait()
        return carry

    lax.fori_loop(0, REQ, begin, 0)
    lax.fori_loop(0, REQ, finish, 0)


def spread_slabs(table, slabs, spread):
    tiles = ENC_PAD // HD
    rows = []
    for i in range(REQ):
        slab = slabs[i]
        even = jnp.concatenate([slab[t * HALF:(t + 1) * HALF] for t in range(tiles)], axis=1)
        odd = jnp.concatenate([even[:, SHIFT:], even[:, :SHIFT]], axis=1)
        rows.append(jnp.where(table[2, i] == 1, odd, even))
    stacked = jnp.concatenate(rows, axis=0)
    return jnp.dot(stacked, spread[...], preferred_element_type=jnp.float32).astype(jnp.bfloat16)


def give_kernel(table, c_ref, r_ref, ol_ref, or_ref, l_ref, out_ref, sems):
    fetch(table, REQ, (c_ref, r_ref, ol_ref, or_ref, l_ref), out_ref, sems)


def pick_kernel(table, c_ref, r_ref, ol_ref, or_ref, l_ref, spread, out_ref, slabs, sems):
    fetch(table, 0, (c_ref, r_ref, ol_ref, or_ref, l_ref), slabs, sems)
    out_ref[...] = spread_slabs(table, slabs, spread)


SMEM = pl.BlockSpec(memory_space=pltpu.SMEM)
VMEM = pl.BlockSpec(memory_space=pltpu.VMEM)
ANY = pl.BlockSpec(memory_space=pl.ANY)


def give(table, pieces):
    return pl.pallas_call(
        give_kernel,
        in_specs=[SMEM] + [ANY] * 5,
        out_specs=VMEM,
        out_shape=jax.ShapeDtypeStruct((REQ, SLAB, HD), jnp.bfloat16),
        scratch_shapes=[pltpu.SemaphoreType.DMA((REQ,))],
        compiler_params=pltpu.CompilerParams(vmem_limit_bytes=16 * 2**20),
        name="give_encodings",
    )(table, *pieces)


def pick(table, pieces, spread):
    return pl.pallas_call(
        pick_kernel,
        in_specs=[SMEM] + [ANY] * 5 + [VMEM],
        out_specs=VMEM,
        out_shape=jax.ShapeDtypeStruct((REQ * HALF, ENC_PAD), jnp.bfloat16),
        scratch_shapes=[
            pltpu.VMEM((REQ, SLAB, HD), jnp.bfloat16),
            pltpu.SemaphoreType.DMA((REQ,)),
        ],
        compiler_params=pltpu.CompilerParams(vmem_limit_bytes=32 * 2**20),
        name="pick_encodings",
    )(table, *pieces, spread)


def attend_kernel(
    live, table, own_ref, slabs, spread, w_ref, x_ref, inv_ref, gain_ref, out_ref, other_ref
):

    @pl.when(pl.program_id(0) == 0)
    def _():
        other_ref[...] = spread_slabs(table, slabs, spread)

    own, other = own_ref[...], other_ref[...]
    inv = inv_ref[...]
    groups = x_ref.shape[0] // GROUP
    column = lax.broadcasted_iota(jnp.int32, (1, HD), 1)
    biases = []
    for c in range(groups):
        bias = jnp.where(jnp.where(column < HALF, live[2 * c], live[2 * c + 1]) > 0, 0.0, -1e30)
        biases.append(jnp.broadcast_to(jnp.concatenate([bias, bias], axis=1), (GROUP, 4 * HALF)))
    bias = jnp.concatenate(biases, axis=0)
    for b in range(HB):
        base = b * 2 * W_PAD
        head = slice(b * HD, (b + 1) * HD)
        key_w = jnp.concatenate([w_ref[j, base:base + W_PAD] for j in range(RING)], axis=0)
        value_w = jnp.concatenate([w_ref[j, base + W_PAD:base + 2 * W_PAD] for j in range(RING)], axis=0)
        weight = jnp.concatenate([key_w, value_w], axis=1)
        kv_own = jnp.dot(own, weight, preferred_element_type=jnp.float32).astype(jnp.bfloat16)
        kv_other = jnp.dot(other, weight, preferred_element_type=jnp.float32).astype(jnp.bfloat16)
        x = x_ref[:, head].astype(jnp.float32)
        q = (x * inv * gain_ref[:, head] * HD ** (-0.5)).astype(jnp.bfloat16)
        scores, values = [], []
        for c in range(groups):
            keys = slice(c * 2 * HALF, (c + 1) * 2 * HALF)
            key = jnp.concatenate([kv_own[keys, :HD], kv_other[keys, :HD]], axis=0)
            values.append(jnp.concatenate([kv_own[keys, HD:], kv_other[keys, HD:]], axis=0))
            scores.append(
                lax.dot_general(
                    q[c * GROUP:(c + 1) * GROUP],
                    key,
                    (((1,), (1,)), ((), ())),
                    preferred_element_type=jnp.float32,
                )
            )
        masked = jnp.concatenate(scores, axis=0) + bias
        row_max = jnp.max(masked, axis=1, keepdims=True)
        row_max = jnp.where(row_max > -1e29, row_max, 0.0)
        expo = jnp.exp(masked - row_max)
        total = jnp.maximum(jnp.sum(expo, axis=1, keepdims=True), 1.0)
        probs = (expo * (1.0 / total)).astype(jnp.bfloat16)
        attended = [
            jnp.dot(probs[c * GROUP:(c + 1) * GROUP], values[c], preferred_element_type=jnp.float32)
            for c in range(groups)
        ]
        out_ref[:, head] = (x + jnp.concatenate(attended, axis=0)).astype(jnp.bfloat16)


def attend(live, table, own, slabs, spread, weights, x, inv, gain):
    tokens, width = x.shape
    whole = lambda *shape: pl.BlockSpec(shape, lambda i, live, table: (0,) * len(shape))
    return pl.pallas_call(
        attend_kernel,
        grid_spec=pltpu.PrefetchScalarGridSpec(
            num_scalar_prefetch=2,
            grid=(HEADS_HERE // HB,),
            in_specs=[
                whole(REQ * HALF, ENC_PAD),
                whole(REQ, SLAB, HD),
                whole(ENC_PAD, ENC_PAD),
                pl.BlockSpec((RING, HB * 2 * W_PAD, HD), lambda i, live, table: (0, i, 0)),
                pl.BlockSpec((tokens, HB * HD), lambda i, live, table: (0, i)),
                whole(tokens, 1),
                pl.BlockSpec((1, HB * HD), lambda i, live, table: (0, i)),
            ],
            out_specs=pl.BlockSpec((tokens, HB * HD), lambda i, live, table: (0, i)),
            scratch_shapes=[pltpu.VMEM((REQ * HALF, ENC_PAD), jnp.bfloat16)],
        ),
        out_shape=jax.ShapeDtypeStruct((tokens, width), jnp.bfloat16),
        compiler_params=pltpu.CompilerParams(vmem_limit_bytes=58 * 2**20),
        name="attend_heads",
    )(live, table, own, slabs, spread, weights, x, inv, gain)


def ring_place(owner, core):
    x, y = owner // SIDE, owner % SIDE
    return jnp.where(core == 0, x, y), jnp.where(core == 0, y, x)


def spread_of(core, here):
    channel = jnp.arange(ENC_PAD)
    near, far = ring_place(channel // W_PART, core)
    near = (near - ring_place(here, core)[0]) % SIDE
    place = (far * SIDE + near) * W_PAD + channel % W_PART
    place = lax.optimization_barrier(jnp.where(channel < ENC, place, -1))
    column = lax.broadcasted_iota(jnp.int32, (ENC_PAD, ENC_PAD), 1)
    return (place[:, None] == column).astype(jnp.bfloat16)


def source_table(requests, core, here):
    owner, block = requests // 6, requests % 6
    near, far = ring_place(owner, core)
    far = (far - ring_place(here, core)[1]) % SIDE
    which = jnp.where(far < 2, far, jnp.where(far == 3, 4, jnp.where(near < 2, 2, 3)))
    chunk = jnp.where(which == 3, near - 2, near)
    odd = block % 2
    row = chunk * D_ROWS + (block // 2) * (TILES * HALF) + odd * (TILES - ENC_PAD // HD) * HALF
    return jnp.stack([which, row, odd])


def first_ring(piece):
    groups = ring_groups(lax.axis_size("segment"), 0)
    copies = jnp.tile(piece, (SIDE, 1))
    return lax.all_to_all(
        copies, ("segment", "db"), split_axis=0, concat_axis=0, tiled=True, axis_index_groups=groups
    )


def on_device(stream, gain, key_weight, value_weight, owners, blocks, valid, database):
    core = lax.axis_index("segment") % 2
    place = lax.axis_index("db")
    rows = stream[0]
    tokens, local_width = rows.shape
    full_width = local_width * lax.axis_size("mp")

    def pack_weight(w):
        return jnp.pad(w[0], ((0, W_PAD - W_PART), (0, 0)))

    packed_w = jnp.concatenate([pack_weight(key_weight), pack_weight(value_weight)], axis=0)
    packed_w = packed_w.reshape(2 * W_PAD, HEADS_HERE, HD).transpose(1, 0, 2).reshape(W_ROWS, HD)

    half = lax.dynamic_slice(database, (0, core * HALF, 0), (2 * PAIRS, HALF, ENC))
    paired = jnp.concatenate([half[0::2], half[1::2]], axis=2)
    packed_d = paired.reshape(PAIRS, HALF, TILES, HD).transpose(0, 2, 1, 3).reshape(D_ROWS, HD)

    as_float = rows.astype(jnp.float32)
    squares = jnp.sum(as_float * as_float, axis=1)
    requests = (owners[0] * 6 + blocks[0]).reshape(-1)
    info = jnp.concatenate(
        [squares, gain[0], valid[0].reshape(-1).astype(jnp.float32), requests.astype(jnp.float32)]
    )
    info = jnp.pad(info, (0, -info.shape[0] % 1024)).reshape(-1, HD)

    pieces_w = [to_next_turned(packed_w, turn) for turn in (0, -1, 2, 1)]
    pieces_w[0], line_d, info, requests = lax.optimization_barrier(
        (pieces_w[0], first_ring(packed_d), info, requests)
    )
    all_w = lax.all_gather(
        jnp.concatenate(pieces_w, axis=0),
        ("segment", "db"),
        axis=0,
        tiled=True,
        axis_index_groups=ring_groups(lax.axis_size("segment"), 1),
    ).reshape(RING, W_ROWS, HD)
    d_before, d_after = turned(line_d, 1, 1), turned(line_d, -1, 1)
    info_here = to_next(info).reshape(-1)
    requests_other = to_next_other_core(requests)
    info_here, rows = lax.optimization_barrier((info_here, rows))
    x_here = to_next(rows)
    spread = spread_of(core, place)
    d_before, d_after, spread, requests_other = lax.optimization_barrier((d_before, d_after, spread, requests_other))
    mid_d = line_d.shape[0] // 2
    d_pieces = (line_d, d_after, turned(d_before[:mid_d], 1, 1), turned(d_after[mid_d:], -1, 1), d_before)

    squares_here = info_here[:tokens]
    squares_other = other_mp(squares_here.reshape(-1, HD)).reshape(-1)
    gain_here = info_here[tokens:tokens + local_width]
    ints = info_here[tokens + local_width:tokens + local_width + 2 * REQ].astype(jnp.int32)
    live, requests_here = ints[:REQ], ints[REQ:]
    table = jnp.concatenate(
        [source_table(requests_here, core, place), source_table(requests_other, core, place)], axis=1
    )

    given, squares_other, x_here = lax.optimization_barrier((give(table, d_pieces), squares_other, x_here))
    slabs = other_core(given)
    own = pick(table, d_pieces, spread)
    inv_rms = lax.rsqrt((squares_here + squares_other) / full_width + eps_norm)
    updated = attend(live, table, own, slabs, spread, all_w, x_here, inv_rms[:, None], gain_here[None, :])
    return updated[None]


def solution(mesh):
    return jax.shard_map(
        on_device,
        mesh=mesh,
        in_specs=(
            P("segment", "db", "mp"),
            P("segment", "mp"),
            P("segment", "db", "mp"),
            P("segment", "db", "mp"),
            P("segment", "db", None),
            P("segment", "db", None),
            P("segment", "db", None),
            P("db", None, None),
        ),
        out_specs=P("segment", "db", "mp"),
        check_vma=False,
    )
```

```python
import jax
import jax.numpy as jnp
from jax import lax
from jax.experimental import pallas as pl
from jax.experimental.pallas import tpu as pltpu
from jax.sharding import PartitionSpec as P

HD = 128
GROUP = 64
SIDE = 4
RING = SIDE * SIDE
eps_norm = 1e-06

W_PART = 28
W_PAD = 32
HEADS_HERE = 16
W_ROWS = HEADS_HERE * 2 * W_PAD
ENC = 448
ENC_PAD = RING * W_PAD
SHIFT = ENC_PAD - ENC
HALF = 64
TILES = 2 * ENC // HD
PAIRS = 3
D_ROWS = PAIRS * TILES * HALF
SLAB = ENC_PAD // HD * HALF
REQ = 12
HB = 4


def ring_pairs(segments, turn, along_x_core):
    pairs = []
    for seg in range(segments):
        for place in range(RING):
            x, y = divmod(place, SIDE)
            if seg % 2 == along_x_core:
                to = ((x + turn) % SIDE) * SIDE + y
            else:
                to = x * SIDE + (y + turn) % SIDE
            pairs.append((seg * RING + place, seg * RING + to))
    return pairs


def ring_groups(segments, along_x_core):
    groups = []
    for seg in range(segments):
        for line in range(SIDE):
            if seg % 2 == along_x_core:
                groups.append([seg * RING + x * SIDE + line for x in range(SIDE)])
            else:
                groups.append([seg * RING + line * SIDE + y for y in range(SIDE)])
    return groups


def turned(value, turn, along_x_core):
    pairs = ring_pairs(lax.axis_size("segment"), turn, along_x_core)
    return lax.ppermute(value, ("segment", "db"), pairs)


def to_next_turned(value, turn):
    count = lax.axis_size("segment")
    behind = ring_pairs(count, turn, 0)
    pairs = [(((seg - 1) % count) * RING + place, to) for seg in range(count) for place, to in
             [(source % RING, target) for source, target in behind[seg * RING:(seg + 1) * RING]]]
    return lax.ppermute(value, ("segment", "db"), pairs)


def to_next(value):
    count = lax.axis_size("segment")
    return lax.ppermute(value, "segment", [(s, (s + 1) % count) for s in range(count)])


def to_next_other_core(value):
    count = lax.axis_size("segment")
    return lax.ppermute(value, "segment", [(s, ((s + 1) % count) ^ 1) for s in range(count)])


def other_mp(value):
    return lax.ppermute(value, "mp", [(0, 1), (1, 0)])


def other_core(value):
    count = lax.axis_size("segment")
    return lax.ppermute(value, "segment", [(s, s ^ 1) for s in range(count)])


def fetch(table, first, sources, slabs, sems):
    def begin(i, carry):
        which = table[0, first + i]
        row = pl.multiple_of(table[1, first + i], 64)
        for number, source in enumerate(sources):
            @pl.when(which == number)
            def _():
                pltpu.make_async_copy(source.at[pl.ds(row, SLAB)], slabs.at[i], sems.at[i]).start()
        return carry

    def finish(i, carry):
        pltpu.make_async_copy(sources[0].at[pl.ds(0, SLAB)], slabs.at[i], sems.at[i]).wait()
        return carry

    lax.fori_loop(0, REQ, begin, 0)
    lax.fori_loop(0, REQ, finish, 0)


def spread_slabs(table, slabs, spread):
    tiles = ENC_PAD // HD
    rows = []
    for i in range(REQ):
        slab = slabs[i]
        even = jnp.concatenate([slab[t * HALF:(t + 1) * HALF] for t in range(tiles)], axis=1)
        odd = jnp.concatenate([even[:, SHIFT:], even[:, :SHIFT]], axis=1)
        rows.append(jnp.where(table[2, i] == 1, odd, even))
    stacked = jnp.concatenate(rows, axis=0)
    return jnp.dot(stacked, spread[...], preferred_element_type=jnp.float32).astype(jnp.bfloat16)


def give_kernel(table, c_ref, r_ref, ol_ref, or_ref, l_ref, out_ref, sems):
    fetch(table, REQ, (c_ref, r_ref, ol_ref, or_ref, l_ref), out_ref, sems)


def pick_kernel(table, c_ref, r_ref, ol_ref, or_ref, l_ref, spread, out_ref, slabs, sems):
    fetch(table, 0, (c_ref, r_ref, ol_ref, or_ref, l_ref), slabs, sems)
    out_ref[...] = spread_slabs(table, slabs, spread)


SMEM = pl.BlockSpec(memory_space=pltpu.SMEM)
VMEM = pl.BlockSpec(memory_space=pltpu.VMEM)
ANY = pl.BlockSpec(memory_space=pl.ANY)


def give(table, pieces):
    return pl.pallas_call(
        give_kernel,
        in_specs=[SMEM] + [ANY] * 5,
        out_specs=VMEM,
        out_shape=jax.ShapeDtypeStruct((REQ, SLAB, HD), jnp.bfloat16),
        scratch_shapes=[pltpu.SemaphoreType.DMA((REQ,))],
        compiler_params=pltpu.CompilerParams(vmem_limit_bytes=16 * 2**20),
        name="give_encodings",
    )(table, *pieces)


def pick(table, pieces, spread):
    return pl.pallas_call(
        pick_kernel,
        in_specs=[SMEM] + [ANY] * 5 + [VMEM],
        out_specs=VMEM,
        out_shape=jax.ShapeDtypeStruct((REQ * HALF, ENC_PAD), jnp.bfloat16),
        scratch_shapes=[
            pltpu.VMEM((REQ, SLAB, HD), jnp.bfloat16),
            pltpu.SemaphoreType.DMA((REQ,)),
        ],
        compiler_params=pltpu.CompilerParams(vmem_limit_bytes=32 * 2**20),
        name="pick_encodings",
    )(table, *pieces, spread)


def attend_kernel(
    live, table, own_ref, slabs, spread, w_ref, x_ref, inv_ref, gain_ref, out_ref, other_ref
):

    @pl.when(pl.program_id(0) == 0)
    def _():
        other_ref[...] = spread_slabs(table, slabs, spread)

    own, other = own_ref[...], other_ref[...]
    inv = inv_ref[...]
    groups = x_ref.shape[0] // GROUP
    column = lax.broadcasted_iota(jnp.int32, (1, HD), 1)
    biases = []
    for c in range(groups):
        bias = jnp.where(jnp.where(column < HALF, live[2 * c], live[2 * c + 1]) > 0, 0.0, -1e30)
        biases.append(jnp.broadcast_to(jnp.concatenate([bias, bias], axis=1), (GROUP, 4 * HALF)))
    bias = jnp.concatenate(biases, axis=0)
    for b in range(HB):
        base = b * 2 * W_PAD
        head = slice(b * HD, (b + 1) * HD)
        key_w = jnp.concatenate([w_ref[j, base:base + W_PAD] for j in range(RING)], axis=0)
        value_w = jnp.concatenate([w_ref[j, base + W_PAD:base + 2 * W_PAD] for j in range(RING)], axis=0)
        weight = jnp.concatenate([key_w, value_w], axis=1)
        kv_own = jnp.dot(own, weight, preferred_element_type=jnp.float32).astype(jnp.bfloat16)
        kv_other = jnp.dot(other, weight, preferred_element_type=jnp.float32).astype(jnp.bfloat16)
        x = x_ref[:, head].astype(jnp.float32)
        q = (x * inv * gain_ref[:, head] * HD ** (-0.5)).astype(jnp.bfloat16)
        scores, values = [], []
        for c in range(groups):
            keys = slice(c * 2 * HALF, (c + 1) * 2 * HALF)
            key = jnp.concatenate([kv_own[keys, :HD], kv_other[keys, :HD]], axis=0)
            values.append(jnp.concatenate([kv_own[keys, HD:], kv_other[keys, HD:]], axis=0))
            scores.append(
                lax.dot_general(
                    q[c * GROUP:(c + 1) * GROUP],
                    key,
                    (((1,), (1,)), ((), ())),
                    preferred_element_type=jnp.float32,
                )
            )
        masked = jnp.concatenate(scores, axis=0) + bias
        row_max = jnp.max(masked, axis=1, keepdims=True)
        row_max = jnp.where(row_max > -1e29, row_max, 0.0)
        expo = jnp.exp(masked - row_max)
        total = jnp.maximum(jnp.sum(expo, axis=1, keepdims=True), 1.0)
        probs = (expo * (1.0 / total)).astype(jnp.bfloat16)
        attended = [
            jnp.dot(probs[c * GROUP:(c + 1) * GROUP], values[c], preferred_element_type=jnp.float32)
            for c in range(groups)
        ]
        out_ref[:, head] = (x + jnp.concatenate(attended, axis=0)).astype(jnp.bfloat16)


def attend(live, table, own, slabs, spread, weights, x, inv, gain):
    tokens, width = x.shape
    whole = lambda *shape: pl.BlockSpec(shape, lambda i, live, table: (0,) * len(shape))
    return pl.pallas_call(
        attend_kernel,
        grid_spec=pltpu.PrefetchScalarGridSpec(
            num_scalar_prefetch=2,
            grid=(HEADS_HERE // HB,),
            in_specs=[
                whole(REQ * HALF, ENC_PAD),
                whole(REQ, SLAB, HD),
                whole(ENC_PAD, ENC_PAD),
                pl.BlockSpec((RING, HB * 2 * W_PAD, HD), lambda i, live, table: (0, i, 0)),
                pl.BlockSpec((tokens, HB * HD), lambda i, live, table: (0, i)),
                whole(tokens, 1),
                pl.BlockSpec((1, HB * HD), lambda i, live, table: (0, i)),
            ],
            out_specs=pl.BlockSpec((tokens, HB * HD), lambda i, live, table: (0, i)),
            scratch_shapes=[pltpu.VMEM((REQ * HALF, ENC_PAD), jnp.bfloat16)],
        ),
        out_shape=jax.ShapeDtypeStruct((tokens, width), jnp.bfloat16),
        compiler_params=pltpu.CompilerParams(vmem_limit_bytes=58 * 2**20),
        name="attend_heads",
    )(live, table, own, slabs, spread, weights, x, inv, gain)


def ring_place(owner, core):
    x, y = owner // SIDE, owner % SIDE
    return jnp.where(core == 0, x, y), jnp.where(core == 0, y, x)


def spread_of(core, here):
    channel = jnp.arange(ENC_PAD)
    near, far = ring_place(channel // W_PART, core)
    near = (near - ring_place(here, core)[0]) % SIDE
    place = (far * SIDE + near) * W_PAD + channel % W_PART
    place = lax.optimization_barrier(jnp.where(channel < ENC, place, -1))
    column = lax.broadcasted_iota(jnp.int32, (ENC_PAD, ENC_PAD), 1)
    return (place[:, None] == column).astype(jnp.bfloat16)


def source_table(requests, core, here):
    owner, block = requests // 6, requests % 6
    near, far = ring_place(owner, core)
    far = (far - ring_place(here, core)[1]) % SIDE
    which = jnp.where(far < 2, far, jnp.where(far == 3, 4, jnp.where(near < 2, 2, 3)))
    chunk = jnp.where(which == 3, near - 2, near)
    odd = block % 2
    row = chunk * D_ROWS + (block // 2) * (TILES * HALF) + odd * (TILES - ENC_PAD // HD) * HALF
    return jnp.stack([which, row, odd])


def first_ring(piece):
    groups = ring_groups(lax.axis_size("segment"), 0)
    copies = jnp.tile(piece, (SIDE, 1))
    return lax.all_to_all(
        copies, ("segment", "db"), split_axis=0, concat_axis=0, tiled=True, axis_index_groups=groups
    )


def on_device(stream, gain, key_weight, value_weight, owners, blocks, valid, database):
    core = lax.axis_index("segment") % 2
    place = lax.axis_index("db")
    rows = stream[0]
    tokens, local_width = rows.shape
    full_width = local_width * lax.axis_size("mp")

    def pack_weight(w):
        return jnp.pad(w[0], ((0, W_PAD - W_PART), (0, 0)))

    packed_w = jnp.concatenate([pack_weight(key_weight), pack_weight(value_weight)], axis=0)
    packed_w = packed_w.reshape(2 * W_PAD, HEADS_HERE, HD).transpose(1, 0, 2).reshape(W_ROWS, HD)

    half = lax.dynamic_slice(database, (0, core * HALF, 0), (2 * PAIRS, HALF, ENC))
    paired = jnp.concatenate([half[0::2], half[1::2]], axis=2)
    packed_d = paired.reshape(PAIRS, HALF, TILES, HD).transpose(0, 2, 1, 3).reshape(D_ROWS, HD)

    as_float = rows.astype(jnp.float32)
    squares = jnp.sum(as_float * as_float, axis=1)
    requests = (owners[0] * 6 + blocks[0]).reshape(-1)
    info = jnp.concatenate(
        [squares, gain[0], valid[0].reshape(-1).astype(jnp.float32), requests.astype(jnp.float32)]
    )
    info = jnp.pad(info, (0, -info.shape[0] % 1024)).reshape(-1, HD)

    pieces_w = [to_next_turned(packed_w, turn) for turn in (0, -1, 2, 1)]
    pieces_w[0], line_d, info, requests = lax.optimization_barrier(
        (pieces_w[0], first_ring(packed_d), info, requests)
    )
    all_w = lax.all_gather(
        jnp.concatenate(pieces_w, axis=0),
        ("segment", "db"),
        axis=0,
        tiled=True,
        axis_index_groups=ring_groups(lax.axis_size("segment"), 1),
    ).reshape(RING, W_ROWS, HD)
    d_before, d_after = turned(line_d, 1, 1), turned(line_d, -1, 1)
    info_here = to_next(info).reshape(-1)
    requests_other = to_next_other_core(requests)
    info_here, requests_other, rows = lax.optimization_barrier((info_here, requests_other, rows))
    x_here = to_next(rows)
    spread = spread_of(core, place)
    d_before, d_after, spread, requests_other = lax.optimization_barrier((d_before, d_after, spread, requests_other))
    mid_d = line_d.shape[0] // 2
    d_pieces = (line_d, d_after, turned(d_before[:mid_d], 1, 1), turned(d_after[mid_d:], -1, 1), d_before)

    squares_here = info_here[:tokens]
    squares_other = other_mp(squares_here.reshape(-1, HD)).reshape(-1)
    gain_here = info_here[tokens:tokens + local_width]
    ints = info_here[tokens + local_width:tokens + local_width + 2 * REQ].astype(jnp.int32)
    live, requests_here = ints[:REQ], ints[REQ:]
    table = jnp.concatenate(
        [source_table(requests_here, core, place), source_table(requests_other, core, place)], axis=1
    )

    given, squares_other, x_here = lax.optimization_barrier((give(table, d_pieces), squares_other, x_here))
    slabs = other_core(given)
    own = pick(table, d_pieces, spread)
    inv_rms = lax.rsqrt((squares_here + squares_other) / full_width + eps_norm)
    updated = attend(live, table, own, slabs, spread, all_w, x_here, inv_rms[:, None], gain_here[None, :])
    return updated[None]


def solution(mesh):
    return jax.shard_map(
        on_device,
        mesh=mesh,
        in_specs=(
            P("segment", "db", "mp"),
            P("segment", "mp"),
            P("segment", "db", "mp"),
            P("segment", "db", "mp"),
            P("segment", "db", None),
            P("segment", "db", None),
            P("segment", "db", None),
            P("db", None, None),
        ),
        out_specs=P("segment", "db", "mp"),
        check_vma=False,
    )
```

```python
import jax
import jax.numpy as jnp
from jax import lax
from jax.experimental import pallas as pl
from jax.experimental.pallas import tpu as pltpu
from jax.sharding import PartitionSpec as P

HD = 128
GROUP = 64
SIDE = 4
RING = SIDE * SIDE
eps_norm = 1e-06

W_PART = 28
W_PAD = 32
HEADS_HERE = 16
W_ROWS = HEADS_HERE * 2 * W_PAD
ENC = 448
ENC_PAD = RING * W_PAD
SHIFT = ENC_PAD - ENC
HALF = 64
TILES = 2 * ENC // HD
PAIRS = 3
D_ROWS = PAIRS * TILES * HALF
SLAB = ENC_PAD // HD * HALF
REQ = 12
HB = 4


def ring_pairs(segments, turn, along_x_core):
    pairs = []
    for seg in range(segments):
        for place in range(RING):
            x, y = divmod(place, SIDE)
            if seg % 2 == along_x_core:
                to = ((x + turn) % SIDE) * SIDE + y
            else:
                to = x * SIDE + (y + turn) % SIDE
            pairs.append((seg * RING + place, seg * RING + to))
    return pairs


def ring_groups(segments, along_x_core):
    groups = []
    for seg in range(segments):
        for line in range(SIDE):
            if seg % 2 == along_x_core:
                groups.append([seg * RING + x * SIDE + line for x in range(SIDE)])
            else:
                groups.append([seg * RING + line * SIDE + y for y in range(SIDE)])
    return groups


def turned(value, turn, along_x_core):
    pairs = ring_pairs(lax.axis_size("segment"), turn, along_x_core)
    return lax.ppermute(value, ("segment", "db"), pairs)


def to_next_turned(value, turn):
    count = lax.axis_size("segment")
    behind = ring_pairs(count, turn, 0)
    pairs = [(((seg - 1) % count) * RING + place, to) for seg in range(count) for place, to in
             [(source % RING, target) for source, target in behind[seg * RING:(seg + 1) * RING]]]
    return lax.ppermute(value, ("segment", "db"), pairs)


def to_next(value):
    count = lax.axis_size("segment")
    return lax.ppermute(value, "segment", [(s, (s + 1) % count) for s in range(count)])


def to_next_other_mp(value):
    count = lax.axis_size("segment")
    pairs = [(s * 2 + m, ((s + 1) % count) * 2 + 1 - m) for s in range(count) for m in range(2)]
    return lax.ppermute(value, ("segment", "mp"), pairs)


def other_core(value):
    count = lax.axis_size("segment")
    return lax.ppermute(value, "segment", [(s, s ^ 1) for s in range(count)])


def fetch(table, first, sources, slabs, sems):
    def begin(i, carry):
        which = table[0, first + i]
        row = pl.multiple_of(table[1, first + i], 64)
        for number, source in enumerate(sources):
            @pl.when(which == number)
            def _():
                pltpu.make_async_copy(source.at[pl.ds(row, SLAB)], slabs.at[i], sems.at[i]).start()
        return carry

    def finish(i, carry):
        pltpu.make_async_copy(sources[0].at[pl.ds(0, SLAB)], slabs.at[i], sems.at[i]).wait()
        return carry

    lax.fori_loop(0, REQ, begin, 0)
    lax.fori_loop(0, REQ, finish, 0)


def spread_slabs(table, slabs, spread):
    tiles = ENC_PAD // HD
    rows = []
    for i in range(REQ):
        slab = slabs[i]
        even = jnp.concatenate([slab[t * HALF:(t + 1) * HALF] for t in range(tiles)], axis=1)
        odd = jnp.concatenate([even[:, SHIFT:], even[:, :SHIFT]], axis=1)
        rows.append(jnp.where(table[2, i] == 1, odd, even))
    stacked = jnp.concatenate(rows, axis=0)
    return jnp.dot(stacked, spread[...], preferred_element_type=jnp.float32).astype(jnp.bfloat16)


def give_kernel(table, c_ref, r_ref, ol_ref, or_ref, l_ref, out_ref, sems):
    fetch(table, REQ, (c_ref, r_ref, ol_ref, or_ref, l_ref), out_ref, sems)


def pick_kernel(table, c_ref, r_ref, ol_ref, or_ref, l_ref, spread, out_ref, slabs, sems):
    fetch(table, 0, (c_ref, r_ref, ol_ref, or_ref, l_ref), slabs, sems)
    out_ref[...] = spread_slabs(table, slabs, spread)


SMEM = pl.BlockSpec(memory_space=pltpu.SMEM)
VMEM = pl.BlockSpec(memory_space=pltpu.VMEM)
ANY = pl.BlockSpec(memory_space=pl.ANY)


def give(table, pieces):
    return pl.pallas_call(
        give_kernel,
        in_specs=[SMEM] + [ANY] * 5,
        out_specs=VMEM,
        out_shape=jax.ShapeDtypeStruct((REQ, SLAB, HD), jnp.bfloat16),
        scratch_shapes=[pltpu.SemaphoreType.DMA((REQ,))],
        compiler_params=pltpu.CompilerParams(vmem_limit_bytes=16 * 2**20),
        name="give_encodings",
    )(table, *pieces)


def pick(table, pieces, spread):
    return pl.pallas_call(
        pick_kernel,
        in_specs=[SMEM] + [ANY] * 5 + [VMEM],
        out_specs=VMEM,
        out_shape=jax.ShapeDtypeStruct((REQ * HALF, ENC_PAD), jnp.bfloat16),
        scratch_shapes=[
            pltpu.VMEM((REQ, SLAB, HD), jnp.bfloat16),
            pltpu.SemaphoreType.DMA((REQ,)),
        ],
        compiler_params=pltpu.CompilerParams(vmem_limit_bytes=32 * 2**20),
        name="pick_encodings",
    )(table, *pieces, spread)


def attend_kernel(
    live, table, own_ref, slabs, spread, w_ref, x_ref, inv_ref, gain_ref, out_ref, other_ref
):

    @pl.when(pl.program_id(0) == 0)
    def _():
        other_ref[...] = spread_slabs(table, slabs, spread)

    own, other = own_ref[...], other_ref[...]
    inv = inv_ref[...]
    groups = x_ref.shape[0] // GROUP
    column = lax.broadcasted_iota(jnp.int32, (1, HD), 1)
    biases = []
    for c in range(groups):
        bias = jnp.where(jnp.where(column < HALF, live[2 * c], live[2 * c + 1]) > 0, 0.0, -1e30)
        biases.append(jnp.broadcast_to(jnp.concatenate([bias, bias], axis=1), (GROUP, 4 * HALF)))
    bias = jnp.concatenate(biases, axis=0)
    for b in range(HB):
        base = b * 2 * W_PAD
        head = slice(b * HD, (b + 1) * HD)
        key_w = jnp.concatenate([w_ref[j, base:base + W_PAD] for j in range(RING)], axis=0)
        value_w = jnp.concatenate([w_ref[j, base + W_PAD:base + 2 * W_PAD] for j in range(RING)], axis=0)
        weight = jnp.concatenate([key_w, value_w], axis=1)
        kv_own = jnp.dot(own, weight, preferred_element_type=jnp.float32).astype(jnp.bfloat16)
        kv_other = jnp.dot(other, weight, preferred_element_type=jnp.float32).astype(jnp.bfloat16)
        x = x_ref[:, head].astype(jnp.float32)
        q = (x * inv * gain_ref[:, head] * HD ** (-0.5)).astype(jnp.bfloat16)
        scores, values = [], []
        for c in range(groups):
            keys = slice(c * 2 * HALF, (c + 1) * 2 * HALF)
            key = jnp.concatenate([kv_own[keys, :HD], kv_other[keys, :HD]], axis=0)
            values.append(jnp.concatenate([kv_own[keys, HD:], kv_other[keys, HD:]], axis=0))
            scores.append(
                lax.dot_general(
                    q[c * GROUP:(c + 1) * GROUP],
                    key,
                    (((1,), (1,)), ((), ())),
                    preferred_element_type=jnp.float32,
                )
            )
        masked = jnp.concatenate(scores, axis=0) + bias
        row_max = jnp.max(masked, axis=1, keepdims=True)
        row_max = jnp.where(row_max > -1e29, row_max, 0.0)
        expo = jnp.exp(masked - row_max)
        total = jnp.maximum(jnp.sum(expo, axis=1, keepdims=True), 1.0)
        probs = (expo * (1.0 / total)).astype(jnp.bfloat16)
        attended = [
            jnp.dot(probs[c * GROUP:(c + 1) * GROUP], values[c], preferred_element_type=jnp.float32)
            for c in range(groups)
        ]
        out_ref[:, head] = (x + jnp.concatenate(attended, axis=0)).astype(jnp.bfloat16)


def attend(live, table, own, slabs, spread, weights, x, inv, gain):
    tokens, width = x.shape
    whole = lambda *shape: pl.BlockSpec(shape, lambda i, live, table: (0,) * len(shape))
    return pl.pallas_call(
        attend_kernel,
        grid_spec=pltpu.PrefetchScalarGridSpec(
            num_scalar_prefetch=2,
            grid=(HEADS_HERE // HB,),
            in_specs=[
                whole(REQ * HALF, ENC_PAD),
                whole(REQ, SLAB, HD),
                whole(ENC_PAD, ENC_PAD),
                pl.BlockSpec((RING, HB * 2 * W_PAD, HD), lambda i, live, table: (0, i, 0)),
                pl.BlockSpec((tokens, HB * HD), lambda i, live, table: (0, i)),
                whole(tokens, 1),
                pl.BlockSpec((1, HB * HD), lambda i, live, table: (0, i)),
            ],
            out_specs=pl.BlockSpec((tokens, HB * HD), lambda i, live, table: (0, i)),
            scratch_shapes=[pltpu.VMEM((REQ * HALF, ENC_PAD), jnp.bfloat16)],
        ),
        out_shape=jax.ShapeDtypeStruct((tokens, width), jnp.bfloat16),
        compiler_params=pltpu.CompilerParams(vmem_limit_bytes=58 * 2**20),
        name="attend_heads",
    )(live, table, own, slabs, spread, weights, x, inv, gain)


def ring_place(owner, core):
    x, y = owner // SIDE, owner % SIDE
    return jnp.where(core == 0, x, y), jnp.where(core == 0, y, x)


def spread_of(core, here):
    channel = jnp.arange(ENC_PAD)
    near, far = ring_place(channel // W_PART, core)
    near = (near - ring_place(here, core)[0]) % SIDE
    place = (far * SIDE + near) * W_PAD + channel % W_PART
    place = lax.optimization_barrier(jnp.where(channel < ENC, place, -1))
    column = lax.broadcasted_iota(jnp.int32, (ENC_PAD, ENC_PAD), 1)
    return (place[:, None] == column).astype(jnp.bfloat16)


def source_table(requests, core, here):
    owner, block = requests // 6, requests % 6
    near, far = ring_place(owner, core)
    far = (far - ring_place(here, core)[1]) % SIDE
    which = jnp.where(far < 2, far, jnp.where(far == 3, 4, jnp.where(near < 2, 2, 3)))
    chunk = jnp.where(which == 3, near - 2, near)
    odd = block % 2
    row = chunk * D_ROWS + (block // 2) * (TILES * HALF) + odd * (TILES - ENC_PAD // HD) * HALF
    return jnp.stack([which, row, odd])


def first_ring(piece):
    groups = ring_groups(lax.axis_size("segment"), 0)
    copies = jnp.tile(piece, (SIDE, 1))
    return lax.all_to_all(
        copies, ("segment", "db"), split_axis=0, concat_axis=0, tiled=True, axis_index_groups=groups
    )


def on_device(stream, gain, key_weight, value_weight, owners, blocks, valid, database):
    core = lax.axis_index("segment") % 2
    place = lax.axis_index("db")
    rows = stream[0]
    tokens, local_width = rows.shape
    full_width = local_width * lax.axis_size("mp")

    def pack_weight(w):
        return jnp.pad(w[0], ((0, W_PAD - W_PART), (0, 0)))

    packed_w = jnp.concatenate([pack_weight(key_weight), pack_weight(value_weight)], axis=0)
    packed_w = packed_w.reshape(2 * W_PAD, HEADS_HERE, HD).transpose(1, 0, 2).reshape(W_ROWS, HD)

    half = lax.dynamic_slice(database, (0, core * HALF, 0), (2 * PAIRS, HALF, ENC))
    paired = jnp.concatenate([half[0::2], half[1::2]], axis=2)
    packed_d = paired.reshape(PAIRS, HALF, TILES, HD).transpose(0, 2, 1, 3).reshape(D_ROWS, HD)

    as_float = rows.astype(jnp.float32)
    squares = jnp.sum(as_float * as_float, axis=1)
    requests = (owners[0] * 6 + blocks[0]).reshape(-1)
    info = jnp.concatenate(
        [squares, gain[0], valid[0].reshape(-1).astype(jnp.float32), requests.astype(jnp.float32)]
    )
    info = jnp.pad(info, (0, -info.shape[0] % 1024)).reshape(-1, HD)

    pieces_w = [to_next_turned(packed_w, turn) for turn in (0, -1, 2, 1)]
    pieces_w[0], line_d, info, squares = lax.optimization_barrier(
        (pieces_w[0], first_ring(packed_d), info, squares)
    )
    all_w = lax.all_gather(
        jnp.concatenate(pieces_w, axis=0),
        ("segment", "db"),
        axis=0,
        tiled=True,
        axis_index_groups=ring_groups(lax.axis_size("segment"), 1),
    ).reshape(RING, W_ROWS, HD)
    d_before, d_after = turned(line_d, 1, 1), turned(line_d, -1, 1)
    info_here = to_next(info).reshape(-1)
    squares_other = to_next_other_mp(squares.reshape(-1, HD)).reshape(-1)
    squares_here = info_here[:tokens]
    gain_here = info_here[tokens:tokens + local_width]
    ints = info_here[tokens + local_width:tokens + local_width + 2 * REQ].astype(jnp.int32)
    live, requests_here = ints[:REQ], ints[REQ:]
    requests_other = other_core(requests_here)
    requests_other, squares_other, rows = lax.optimization_barrier((requests_other, squares_other, rows))
    x_here = to_next(rows)
    spread = spread_of(core, place)
    d_before, d_after, spread, requests_other = lax.optimization_barrier((d_before, d_after, spread, requests_other))
    mid_d = line_d.shape[0] // 2
    d_pieces = (line_d, d_after, turned(d_before[:mid_d], 1, 1), turned(d_after[mid_d:], -1, 1), d_before)

    table = jnp.concatenate(
        [source_table(requests_here, core, place), source_table(requests_other, core, place)], axis=1
    )

    given, x_here = lax.optimization_barrier((give(table, d_pieces), x_here))
    slabs = other_core(given)
    own = pick(table, d_pieces, spread)
    inv_rms = lax.rsqrt((squares_here + squares_other) / full_width + eps_norm)
    updated = attend(live, table, own, slabs, spread, all_w, x_here, inv_rms[:, None], gain_here[None, :])
    return updated[None]


def solution(mesh):
    return jax.shard_map(
        on_device,
        mesh=mesh,
        in_specs=(
            P("segment", "db", "mp"),
            P("segment", "mp"),
            P("segment", "db", "mp"),
            P("segment", "db", "mp"),
            P("segment", "db", None),
            P("segment", "db", None),
            P("segment", "db", None),
            P("db", None, None),
        ),
        out_specs=P("segment", "db", "mp"),
        check_vma=False,
    )
```

```python
import jax
import jax.numpy as jnp
from jax import lax
from jax.experimental import pallas as pl
from jax.experimental.pallas import tpu as pltpu
from jax.sharding import PartitionSpec as P

HD = 128
GROUP = 64
SIDE = 4
RING = SIDE * SIDE
eps_norm = 1e-06

W_PART = 28
W_PAD = 32
HEADS_HERE = 16
W_ROWS = HEADS_HERE * 2 * W_PAD
ENC = 448
ENC_PAD = RING * W_PAD
SHIFT = ENC_PAD - ENC
HALF = 64
TILES = 2 * ENC // HD
PAIRS = 3
D_ROWS = PAIRS * TILES * HALF
SLAB = ENC_PAD // HD * HALF
REQ = 12
HB = 4


def ring_pairs(segments, turn, along_x_core):
    pairs = []
    for seg in range(segments):
        for place in range(RING):
            x, y = divmod(place, SIDE)
            if seg % 2 == along_x_core:
                to = ((x + turn) % SIDE) * SIDE + y
            else:
                to = x * SIDE + (y + turn) % SIDE
            pairs.append((seg * RING + place, seg * RING + to))
    return pairs


def ring_groups(segments, along_x_core):
    groups = []
    for seg in range(segments):
        for line in range(SIDE):
            if seg % 2 == along_x_core:
                groups.append([seg * RING + x * SIDE + line for x in range(SIDE)])
            else:
                groups.append([seg * RING + line * SIDE + y for y in range(SIDE)])
    return groups


def turned(value, turn, along_x_core):
    pairs = ring_pairs(lax.axis_size("segment"), turn, along_x_core)
    return lax.ppermute(value, ("segment", "db"), pairs)


def to_next_turned(value, turn):
    count = lax.axis_size("segment")
    behind = ring_pairs(count, turn, 0)
    pairs = [(((seg - 1) % count) * RING + place, to) for seg in range(count) for place, to in
             [(source % RING, target) for source, target in behind[seg * RING:(seg + 1) * RING]]]
    return lax.ppermute(value, ("segment", "db"), pairs)


def to_next(value):
    count = lax.axis_size("segment")
    return lax.ppermute(value, "segment", [(s, (s + 1) % count) for s in range(count)])


def to_next_other_mp(value):
    count = lax.axis_size("segment")
    pairs = [(s * 2 + m, ((s + 1) % count) * 2 + 1 - m) for s in range(count) for m in range(2)]
    return lax.ppermute(value, ("segment", "mp"), pairs)


def other_core(value):
    count = lax.axis_size("segment")
    return lax.ppermute(value, "segment", [(s, s ^ 1) for s in range(count)])


def fetch(table, first, sources, slabs, sems):
    def begin(i, carry):
        which = table[0, first + i]
        row = pl.multiple_of(table[1, first + i], 64)
        for number, source in enumerate(sources):
            @pl.when(which == number)
            def _():
                pltpu.make_async_copy(source.at[pl.ds(row, SLAB)], slabs.at[i], sems.at[i]).start()
        return carry

    def finish(i, carry):
        pltpu.make_async_copy(sources[0].at[pl.ds(0, SLAB)], slabs.at[i], sems.at[i]).wait()
        return carry

    lax.fori_loop(0, REQ, begin, 0)
    lax.fori_loop(0, REQ, finish, 0)


def spread_slabs(table, slabs, spread):
    tiles = ENC_PAD // HD
    rows = []
    for i in range(REQ):
        slab = slabs[i]
        even = jnp.concatenate([slab[t * HALF:(t + 1) * HALF] for t in range(tiles)], axis=1)
        odd = jnp.concatenate([even[:, SHIFT:], even[:, :SHIFT]], axis=1)
        rows.append(jnp.where(table[2, i] == 1, odd, even))
    stacked = jnp.concatenate(rows, axis=0)
    return jnp.dot(stacked, spread[...], preferred_element_type=jnp.float32).astype(jnp.bfloat16)


def give_kernel(table, c_ref, r_ref, ol_ref, or_ref, l_ref, out_ref, sems):
    fetch(table, REQ, (c_ref, r_ref, ol_ref, or_ref, l_ref), out_ref, sems)


def pick_kernel(table, c_ref, r_ref, ol_ref, or_ref, l_ref, spread, out_ref, slabs, sems):
    fetch(table, 0, (c_ref, r_ref, ol_ref, or_ref, l_ref), slabs, sems)
    out_ref[...] = spread_slabs(table, slabs, spread)


SMEM = pl.BlockSpec(memory_space=pltpu.SMEM)
VMEM = pl.BlockSpec(memory_space=pltpu.VMEM)
ANY = pl.BlockSpec(memory_space=pl.ANY)


def give(table, pieces):
    return pl.pallas_call(
        give_kernel,
        in_specs=[SMEM] + [ANY] * 5,
        out_specs=VMEM,
        out_shape=jax.ShapeDtypeStruct((REQ, SLAB, HD), jnp.bfloat16),
        scratch_shapes=[pltpu.SemaphoreType.DMA((REQ,))],
        compiler_params=pltpu.CompilerParams(vmem_limit_bytes=16 * 2**20),
        name="give_encodings",
    )(table, *pieces)


def pick(table, pieces, spread):
    return pl.pallas_call(
        pick_kernel,
        in_specs=[SMEM] + [ANY] * 5 + [VMEM],
        out_specs=VMEM,
        out_shape=jax.ShapeDtypeStruct((REQ * HALF, ENC_PAD), jnp.bfloat16),
        scratch_shapes=[
            pltpu.VMEM((REQ, SLAB, HD), jnp.bfloat16),
            pltpu.SemaphoreType.DMA((REQ,)),
        ],
        compiler_params=pltpu.CompilerParams(vmem_limit_bytes=32 * 2**20),
        name="pick_encodings",
    )(table, *pieces, spread)


def attend_kernel(
    live, table, own_ref, slabs, spread, w_ref, x_ref, inv_ref, gain_ref, out_ref, other_ref
):

    @pl.when(pl.program_id(0) == 0)
    def _():
        other_ref[...] = spread_slabs(table, slabs, spread)

    own, other = own_ref[...], other_ref[...]
    inv = inv_ref[...]
    groups = x_ref.shape[0] // GROUP
    column = lax.broadcasted_iota(jnp.int32, (1, HD), 1)
    biases = []
    for c in range(groups):
        bias = jnp.where(jnp.where(column < HALF, live[2 * c], live[2 * c + 1]) > 0, 0.0, -1e30)
        biases.append(jnp.broadcast_to(jnp.concatenate([bias, bias], axis=1), (GROUP, 4 * HALF)))
    bias = jnp.concatenate(biases, axis=0)
    for b in range(HB):
        base = b * 2 * W_PAD
        head = slice(b * HD, (b + 1) * HD)
        key_w = jnp.concatenate([w_ref[j, base:base + W_PAD] for j in range(RING)], axis=0)
        value_w = jnp.concatenate([w_ref[j, base + W_PAD:base + 2 * W_PAD] for j in range(RING)], axis=0)
        weight = jnp.concatenate([key_w, value_w], axis=1)
        kv_own = jnp.dot(own, weight, preferred_element_type=jnp.float32).astype(jnp.bfloat16)
        kv_other = jnp.dot(other, weight, preferred_element_type=jnp.float32).astype(jnp.bfloat16)
        x = x_ref[:, head].astype(jnp.float32)
        q = (x * inv * gain_ref[:, head] * HD ** (-0.5)).astype(jnp.bfloat16)
        scores, values = [], []
        for c in range(groups):
            keys = slice(c * 2 * HALF, (c + 1) * 2 * HALF)
            key = jnp.concatenate([kv_own[keys, :HD], kv_other[keys, :HD]], axis=0)
            values.append(jnp.concatenate([kv_own[keys, HD:], kv_other[keys, HD:]], axis=0))
            scores.append(
                lax.dot_general(
                    q[c * GROUP:(c + 1) * GROUP],
                    key,
                    (((1,), (1,)), ((), ())),
                    preferred_element_type=jnp.float32,
                )
            )
        masked = jnp.concatenate(scores, axis=0) + bias
        row_max = jnp.max(masked, axis=1, keepdims=True)
        row_max = jnp.where(row_max > -1e29, row_max, 0.0)
        expo = jnp.exp(masked - row_max)
        total = jnp.maximum(jnp.sum(expo, axis=1, keepdims=True), 1.0)
        probs = (expo * (1.0 / total)).astype(jnp.bfloat16)
        attended = [
            jnp.dot(probs[c * GROUP:(c + 1) * GROUP], values[c], preferred_element_type=jnp.float32)
            for c in range(groups)
        ]
        out_ref[:, head] = (x + jnp.concatenate(attended, axis=0)).astype(jnp.bfloat16)


def attend(live, table, own, slabs, spread, weights, x, inv, gain):
    tokens, width = x.shape
    whole = lambda *shape: pl.BlockSpec(shape, lambda i, live, table: (0,) * len(shape))
    return pl.pallas_call(
        attend_kernel,
        grid_spec=pltpu.PrefetchScalarGridSpec(
            num_scalar_prefetch=2,
            grid=(HEADS_HERE // HB,),
            in_specs=[
                whole(REQ * HALF, ENC_PAD),
                whole(REQ, SLAB, HD),
                whole(ENC_PAD, ENC_PAD),
                pl.BlockSpec((RING, HB * 2 * W_PAD, HD), lambda i, live, table: (0, i, 0)),
                pl.BlockSpec((tokens, HB * HD), lambda i, live, table: (0, i)),
                whole(tokens, 1),
                pl.BlockSpec((1, HB * HD), lambda i, live, table: (0, i)),
            ],
            out_specs=pl.BlockSpec((tokens, HB * HD), lambda i, live, table: (0, i)),
            scratch_shapes=[pltpu.VMEM((REQ * HALF, ENC_PAD), jnp.bfloat16)],
        ),
        out_shape=jax.ShapeDtypeStruct((tokens, width), jnp.bfloat16),
        compiler_params=pltpu.CompilerParams(vmem_limit_bytes=58 * 2**20),
        name="attend_heads",
    )(live, table, own, slabs, spread, weights, x, inv, gain)


def ring_place(owner, core):
    x, y = owner // SIDE, owner % SIDE
    return jnp.where(core == 0, x, y), jnp.where(core == 0, y, x)


def spread_of(core, here):
    channel = jnp.arange(ENC_PAD)
    near, far = ring_place(channel // W_PART, core)
    near = (near - ring_place(here, core)[0]) % SIDE
    place = (far * SIDE + near) * W_PAD + channel % W_PART
    place = lax.optimization_barrier(jnp.where(channel < ENC, place, -1))
    column = lax.broadcasted_iota(jnp.int32, (ENC_PAD, ENC_PAD), 1)
    return (place[:, None] == column).astype(jnp.bfloat16)


def source_table(requests, core, here):
    owner, block = requests // 6, requests % 6
    near, far = ring_place(owner, core)
    far = (far - ring_place(here, core)[1]) % SIDE
    which = jnp.where(far < 2, far, jnp.where(far == 3, 4, jnp.where(near < 2, 2, 3)))
    chunk = jnp.where(which == 3, near - 2, near)
    odd = block % 2
    row = chunk * D_ROWS + (block // 2) * (TILES * HALF) + odd * (TILES - ENC_PAD // HD) * HALF
    return jnp.stack([which, row, odd])


def first_ring(piece):
    groups = ring_groups(lax.axis_size("segment"), 0)
    copies = jnp.tile(piece, (SIDE, 1))
    return lax.all_to_all(
        copies, ("segment", "db"), split_axis=0, concat_axis=0, tiled=True, axis_index_groups=groups
    )


def on_device(stream, gain, key_weight, value_weight, owners, blocks, valid, database):
    core = lax.axis_index("segment") % 2
    place = lax.axis_index("db")
    rows = stream[0]
    tokens, local_width = rows.shape
    full_width = local_width * lax.axis_size("mp")

    def pack_weight(w):
        return jnp.pad(w[0], ((0, W_PAD - W_PART), (0, 0)))

    packed_w = jnp.concatenate([pack_weight(key_weight), pack_weight(value_weight)], axis=0)
    packed_w = packed_w.reshape(2 * W_PAD, HEADS_HERE, HD).transpose(1, 0, 2).reshape(W_ROWS, HD)

    half = lax.dynamic_slice(database, (0, core * HALF, 0), (2 * PAIRS, HALF, ENC))
    paired = jnp.concatenate([half[0::2], half[1::2]], axis=2)
    packed_d = paired.reshape(PAIRS, HALF, TILES, HD).transpose(0, 2, 1, 3).reshape(D_ROWS, HD)

    as_float = rows.astype(jnp.float32)
    squares = jnp.sum(as_float * as_float, axis=1)
    requests = (owners[0] * 6 + blocks[0]).reshape(-1)
    info = jnp.concatenate(
        [squares, gain[0], valid[0].reshape(-1).astype(jnp.float32), requests.astype(jnp.float32)]
    )
    info = jnp.pad(info, (0, -info.shape[0] % 1024)).reshape(-1, HD)

    pieces_w = [to_next_turned(packed_w, turn) for turn in (0, -1, 2, 1)]
    pieces_w[0], line_d, info, squares = lax.optimization_barrier(
        (pieces_w[0], first_ring(packed_d), info, squares)
    )
    all_w = lax.all_gather(
        jnp.concatenate(pieces_w, axis=0),
        ("segment", "db"),
        axis=0,
        tiled=True,
        axis_index_groups=ring_groups(lax.axis_size("segment"), 1),
    ).reshape(RING, W_ROWS, HD)
    d_before, d_after = turned(line_d, 1, 1), turned(line_d, -1, 1)
    info_here, rows = lax.optimization_barrier((to_next(info).reshape(-1), rows))
    squares_other = to_next_other_mp(squares.reshape(-1, HD)).reshape(-1)
    squares_here = info_here[:tokens]
    gain_here = info_here[tokens:tokens + local_width]
    ints = info_here[tokens + local_width:tokens + local_width + 2 * REQ].astype(jnp.int32)
    live, requests_here = ints[:REQ], ints[REQ:]
    requests_other = other_core(requests_here)
    x_here = to_next(rows)
    spread = spread_of(core, place)
    d_before, d_after, spread, requests_other = lax.optimization_barrier((d_before, d_after, spread, requests_other))
    mid_d = line_d.shape[0] // 2
    d_pieces = (line_d, d_after, turned(d_before[:mid_d], 1, 1), turned(d_after[mid_d:], -1, 1), d_before)

    table = jnp.concatenate(
        [source_table(requests_here, core, place), source_table(requests_other, core, place)], axis=1
    )

    inv_rms = lax.rsqrt((squares_here + squares_other) / full_width + eps_norm)
    given, x_here, inv_column, gain_row = lax.optimization_barrier(
        (give(table, d_pieces), x_here, inv_rms[:, None], gain_here[None, :])
    )
    slabs = other_core(given)
    own = pick(table, d_pieces, spread)
    updated = attend(live, table, own, slabs, spread, all_w, x_here, inv_column, gain_row)
    return updated[None]


def solution(mesh):
    return jax.shard_map(
        on_device,
        mesh=mesh,
        in_specs=(
            P("segment", "db", "mp"),
            P("segment", "mp"),
            P("segment", "db", "mp"),
            P("segment", "db", "mp"),
            P("segment", "db", None),
            P("segment", "db", None),
            P("segment", "db", None),
            P("db", None, None),
        ),
        out_specs=P("segment", "db", "mp"),
        check_vma=False,
    )
```

```python
import jax
import jax.numpy as jnp
from jax import lax
from jax.experimental import pallas as pl
from jax.experimental.pallas import tpu as pltpu
from jax.sharding import PartitionSpec as P

HD = 128
GROUP = 64
SIDE = 4
RING = SIDE * SIDE
eps_norm = 1e-06

W_PART = 28
W_PAD = 32
HEADS_HERE = 16
W_ROWS = HEADS_HERE * 2 * W_PAD
ENC = 448
ENC_PAD = RING * W_PAD
SHIFT = ENC_PAD - ENC
HALF = 64
TILES = 2 * ENC // HD
PAIRS = 3
D_ROWS = PAIRS * TILES * HALF
SLAB = ENC_PAD // HD * HALF
REQ = 12
HB = 4


def ring_pairs(segments, turn, along_x_core):
    pairs = []
    for seg in range(segments):
        for place in range(RING):
            x, y = divmod(place, SIDE)
            if seg % 2 == along_x_core:
                to = ((x + turn) % SIDE) * SIDE + y
            else:
                to = x * SIDE + (y + turn) % SIDE
            pairs.append((seg * RING + place, seg * RING + to))
    return pairs


def ring_groups(segments, along_x_core):
    groups = []
    for seg in range(segments):
        for line in range(SIDE):
            if seg % 2 == along_x_core:
                groups.append([seg * RING + x * SIDE + line for x in range(SIDE)])
            else:
                groups.append([seg * RING + line * SIDE + y for y in range(SIDE)])
    return groups


def turned(value, turn, along_x_core):
    pairs = ring_pairs(lax.axis_size("segment"), turn, along_x_core)
    return lax.ppermute(value, ("segment", "db"), pairs)


def to_next_turned(value, turn):
    count = lax.axis_size("segment")
    behind = ring_pairs(count, turn, 0)
    pairs = [(((seg - 1) % count) * RING + place, to) for seg in range(count) for place, to in
             [(source % RING, target) for source, target in behind[seg * RING:(seg + 1) * RING]]]
    return lax.ppermute(value, ("segment", "db"), pairs)


def to_next(value):
    count = lax.axis_size("segment")
    return lax.ppermute(value, "segment", [(s, (s + 1) % count) for s in range(count)])


def to_next_other_mp(value):
    count = lax.axis_size("segment")
    pairs = [(s * 2 + m, ((s + 1) % count) * 2 + 1 - m) for s in range(count) for m in range(2)]
    return lax.ppermute(value, ("segment", "mp"), pairs)


def other_core(value):
    count = lax.axis_size("segment")
    return lax.ppermute(value, "segment", [(s, s ^ 1) for s in range(count)])


def fetch(table, first, sources, slabs, sems):
    def begin(i, carry):
        which = table[0, first + i]
        row = pl.multiple_of(table[1, first + i], 64)
        for number, source in enumerate(sources):
            @pl.when(which == number)
            def _():
                pltpu.make_async_copy(source.at[pl.ds(row, SLAB)], slabs.at[i], sems.at[i]).start()
        return carry

    def finish(i, carry):
        pltpu.make_async_copy(sources[0].at[pl.ds(0, SLAB)], slabs.at[i], sems.at[i]).wait()
        return carry

    lax.fori_loop(0, REQ, begin, 0)
    lax.fori_loop(0, REQ, finish, 0)


def spread_slabs(table, slabs, spread):
    tiles = ENC_PAD // HD
    rows = []
    for i in range(REQ):
        slab = slabs[i]
        even = jnp.concatenate([slab[t * HALF:(t + 1) * HALF] for t in range(tiles)], axis=1)
        odd = jnp.concatenate([even[:, SHIFT:], even[:, :SHIFT]], axis=1)
        rows.append(jnp.where(table[2, i] == 1, odd, even))
    stacked = jnp.concatenate(rows, axis=0)
    return jnp.dot(stacked, spread[...], preferred_element_type=jnp.float32).astype(jnp.bfloat16)


def give_kernel(table, c_ref, r_ref, ol_ref, or_ref, l_ref, out_ref, sems):
    fetch(table, REQ, (c_ref, r_ref, ol_ref, or_ref, l_ref), out_ref, sems)


def pick_kernel(table, c_ref, r_ref, ol_ref, or_ref, l_ref, spread, out_ref, slabs, sems):
    fetch(table, 0, (c_ref, r_ref, ol_ref, or_ref, l_ref), slabs, sems)
    out_ref[...] = spread_slabs(table, slabs, spread)


SMEM = pl.BlockSpec(memory_space=pltpu.SMEM)
VMEM = pl.BlockSpec(memory_space=pltpu.VMEM)
ANY = pl.BlockSpec(memory_space=pl.ANY)


def give(table, pieces):
    return pl.pallas_call(
        give_kernel,
        in_specs=[SMEM] + [ANY] * 5,
        out_specs=VMEM,
        out_shape=jax.ShapeDtypeStruct((REQ, SLAB, HD), jnp.bfloat16),
        scratch_shapes=[pltpu.SemaphoreType.DMA((REQ,))],
        compiler_params=pltpu.CompilerParams(vmem_limit_bytes=16 * 2**20),
        name="give_encodings",
    )(table, *pieces)


def pick(table, pieces, spread):
    return pl.pallas_call(
        pick_kernel,
        in_specs=[SMEM] + [ANY] * 5 + [VMEM],
        out_specs=VMEM,
        out_shape=jax.ShapeDtypeStruct((REQ * HALF, ENC_PAD), jnp.bfloat16),
        scratch_shapes=[
            pltpu.VMEM((REQ, SLAB, HD), jnp.bfloat16),
            pltpu.SemaphoreType.DMA((REQ,)),
        ],
        compiler_params=pltpu.CompilerParams(vmem_limit_bytes=32 * 2**20),
        name="pick_encodings",
    )(table, *pieces, spread)


def attend_kernel(
    live, table, own_ref, slabs, spread, w_ref, x_ref, inv_ref, gain_ref, out_ref, other_ref
):

    @pl.when(pl.program_id(0) == 0)
    def _():
        other_ref[...] = spread_slabs(table, slabs, spread)

    own, other = own_ref[...], other_ref[...]
    inv = inv_ref[...]
    groups = x_ref.shape[0] // GROUP
    column = lax.broadcasted_iota(jnp.int32, (1, HD), 1)
    biases = []
    for c in range(groups):
        bias = jnp.where(jnp.where(column < HALF, live[2 * c], live[2 * c + 1]) > 0, 0.0, -1e30)
        biases.append(jnp.broadcast_to(jnp.concatenate([bias, bias], axis=1), (GROUP, 4 * HALF)))
    bias = jnp.concatenate(biases, axis=0)
    for b in range(HB):
        base = b * 2 * W_PAD
        head = slice(b * HD, (b + 1) * HD)
        key_w = jnp.concatenate([w_ref[j, base:base + W_PAD] for j in range(RING)], axis=0)
        value_w = jnp.concatenate([w_ref[j, base + W_PAD:base + 2 * W_PAD] for j in range(RING)], axis=0)
        weight = jnp.concatenate([key_w, value_w], axis=1)
        kv_own = jnp.dot(own, weight, preferred_element_type=jnp.float32).astype(jnp.bfloat16)
        kv_other = jnp.dot(other, weight, preferred_element_type=jnp.float32).astype(jnp.bfloat16)
        x = x_ref[:, head].astype(jnp.float32)
        q = (x * inv * gain_ref[:, head] * HD ** (-0.5)).astype(jnp.bfloat16)
        scores, values = [], []
        for c in range(groups):
            keys = slice(c * 2 * HALF, (c + 1) * 2 * HALF)
            key = jnp.concatenate([kv_own[keys, :HD], kv_other[keys, :HD]], axis=0)
            values.append(jnp.concatenate([kv_own[keys, HD:], kv_other[keys, HD:]], axis=0))
            scores.append(
                lax.dot_general(
                    q[c * GROUP:(c + 1) * GROUP],
                    key,
                    (((1,), (1,)), ((), ())),
                    preferred_element_type=jnp.float32,
                )
            )
        masked = jnp.concatenate(scores, axis=0) + bias
        row_max = jnp.max(masked, axis=1, keepdims=True)
        row_max = jnp.where(row_max > -1e29, row_max, 0.0)
        expo = jnp.exp(masked - row_max)
        total = jnp.maximum(jnp.sum(expo, axis=1, keepdims=True), 1.0)
        probs = (expo * (1.0 / total)).astype(jnp.bfloat16)
        attended = [
            jnp.dot(probs[c * GROUP:(c + 1) * GROUP], values[c], preferred_element_type=jnp.float32)
            for c in range(groups)
        ]
        out_ref[:, head] = (x + jnp.concatenate(attended, axis=0)).astype(jnp.bfloat16)


def attend(live, table, own, slabs, spread, weights, x, inv, gain):
    tokens, width = x.shape
    whole = lambda *shape: pl.BlockSpec(shape, lambda i, live, table: (0,) * len(shape))
    return pl.pallas_call(
        attend_kernel,
        grid_spec=pltpu.PrefetchScalarGridSpec(
            num_scalar_prefetch=2,
            grid=(HEADS_HERE // HB,),
            in_specs=[
                whole(REQ * HALF, ENC_PAD),
                whole(REQ, SLAB, HD),
                whole(ENC_PAD, ENC_PAD),
                pl.BlockSpec((RING, HB * 2 * W_PAD, HD), lambda i, live, table: (0, i, 0)),
                pl.BlockSpec((tokens, HB * HD), lambda i, live, table: (0, i)),
                whole(tokens, 1),
                pl.BlockSpec((1, HB * HD), lambda i, live, table: (0, i)),
            ],
            out_specs=pl.BlockSpec((tokens, HB * HD), lambda i, live, table: (0, i)),
            scratch_shapes=[pltpu.VMEM((REQ * HALF, ENC_PAD), jnp.bfloat16)],
        ),
        out_shape=jax.ShapeDtypeStruct((tokens, width), jnp.bfloat16),
        compiler_params=pltpu.CompilerParams(vmem_limit_bytes=58 * 2**20),
        name="attend_heads",
    )(live, table, own, slabs, spread, weights, x, inv, gain)


def ring_place(owner, core):
    x, y = owner // SIDE, owner % SIDE
    return jnp.where(core == 0, x, y), jnp.where(core == 0, y, x)


def spread_of(core, here):
    channel = jnp.arange(ENC_PAD)
    near, far = ring_place(channel // W_PART, core)
    near = (near - ring_place(here, core)[0]) % SIDE
    place = (far * SIDE + near) * W_PAD + channel % W_PART
    place = lax.optimization_barrier(jnp.where(channel < ENC, place, -1))
    column = lax.broadcasted_iota(jnp.int32, (ENC_PAD, ENC_PAD), 1)
    return (place[:, None] == column).astype(jnp.bfloat16)


def source_table(requests, core, here):
    owner, block = requests // 6, requests % 6
    near, far = ring_place(owner, core)
    far = (far - ring_place(here, core)[1]) % SIDE
    which = jnp.where(far < 2, far, jnp.where(far == 3, 4, jnp.where(near < 2, 2, 3)))
    chunk = jnp.where(which == 3, near - 2, near)
    odd = block % 2
    row = chunk * D_ROWS + (block // 2) * (TILES * HALF) + odd * (TILES - ENC_PAD // HD) * HALF
    return jnp.stack([which, row, odd])


def first_ring(piece):
    groups = ring_groups(lax.axis_size("segment"), 0)
    copies = jnp.tile(piece, (SIDE, 1))
    return lax.all_to_all(
        copies, ("segment", "db"), split_axis=0, concat_axis=0, tiled=True, axis_index_groups=groups
    )


def on_device(stream, gain, key_weight, value_weight, owners, blocks, valid, database):
    core = lax.axis_index("segment") % 2
    place = lax.axis_index("db")
    rows = stream[0]
    tokens, local_width = rows.shape
    full_width = local_width * lax.axis_size("mp")

    def pack_weight(w):
        return jnp.pad(w[0], ((0, W_PAD - W_PART), (0, 0)))

    packed_w = jnp.concatenate([pack_weight(key_weight), pack_weight(value_weight)], axis=0)
    packed_w = packed_w.reshape(2 * W_PAD, HEADS_HERE, HD).transpose(1, 0, 2).reshape(W_ROWS, HD)

    half = lax.dynamic_slice(database, (0, core * HALF, 0), (2 * PAIRS, HALF, ENC))
    paired = jnp.concatenate([half[0::2], half[1::2]], axis=2)
    packed_d = paired.reshape(PAIRS, HALF, TILES, HD).transpose(0, 2, 1, 3).reshape(D_ROWS, HD)

    as_float = rows.astype(jnp.float32)
    squares = jnp.sum(as_float * as_float, axis=1)
    requests = (owners[0] * 6 + blocks[0]).reshape(-1)
    info = jnp.concatenate(
        [squares, gain[0], valid[0].reshape(-1).astype(jnp.float32), requests.astype(jnp.float32)]
    )
    info = jnp.pad(info, (0, -info.shape[0] % 1024)).reshape(-1, HD)

    pieces_w = [to_next_turned(packed_w, turn) for turn in (0, -1, 2, 1)]
    pieces_w[0], line_d, info, squares = lax.optimization_barrier(
        (pieces_w[0], first_ring(packed_d), info, squares)
    )
    all_w = lax.all_gather(
        jnp.concatenate(pieces_w, axis=0),
        ("segment", "db"),
        axis=0,
        tiled=True,
        axis_index_groups=ring_groups(lax.axis_size("segment"), 1),
    ).reshape(RING, W_ROWS, HD)
    d_before, d_after = turned(line_d, 1, 1), turned(line_d, -1, 1)
    info_here = to_next(info).reshape(-1)
    squares_here = info_here[:tokens]
    gain_here = info_here[tokens:tokens + local_width]
    ints = info_here[tokens + local_width:tokens + local_width + 2 * REQ].astype(jnp.int32)
    live, requests_here = ints[:REQ], ints[REQ:]
    requests_other = other_core(requests_here)
    spread = spread_of(core, place)
    d_before, d_after, spread, requests_other, rows, squares = lax.optimization_barrier(
        (d_before, d_after, spread, requests_other, rows, squares)
    )
    x_here = to_next(rows)
    squares_other = to_next_other_mp(squares.reshape(-1, HD)).reshape(-1)
    mid_d = line_d.shape[0] // 2
    d_pieces = (line_d, d_after, turned(d_before[:mid_d], 1, 1), turned(d_after[mid_d:], -1, 1), d_before)

    table = jnp.concatenate(
        [source_table(requests_here, core, place), source_table(requests_other, core, place)], axis=1
    )

    inv_rms = lax.rsqrt((squares_here + squares_other) / full_width + eps_norm)
    given, x_here, inv_column, gain_row = lax.optimization_barrier(
        (give(table, d_pieces), x_here, inv_rms[:, None], gain_here[None, :])
    )
    slabs = other_core(given)
    own = pick(table, d_pieces, spread)
    updated = attend(live, table, own, slabs, spread, all_w, x_here, inv_column, gain_row)
    return updated[None]


def solution(mesh):
    return jax.shard_map(
        on_device,
        mesh=mesh,
        in_specs=(
            P("segment", "db", "mp"),
            P("segment", "mp"),
            P("segment", "db", "mp"),
            P("segment", "db", "mp"),
            P("segment", "db", None),
            P("segment", "db", None),
            P("segment", "db", None),
            P("db", None, None),
        ),
        out_specs=P("segment", "db", "mp"),
        check_vma=False,
    )
```

```python
import jax
import jax.numpy as jnp
from jax import lax
from jax.experimental import pallas as pl
from jax.experimental.pallas import tpu as pltpu
from jax.sharding import PartitionSpec as P

HD = 128
GROUP = 64
SIDE = 4
RING = SIDE * SIDE
eps_norm = 1e-06

W_PART = 28
W_PAD = 32
HEADS_HERE = 16
W_ROWS = HEADS_HERE * 2 * W_PAD
ENC = 448
ENC_PAD = RING * W_PAD
SHIFT = ENC_PAD - ENC
HALF = 64
TILES = 2 * ENC // HD
PAIRS = 3
D_ROWS = PAIRS * TILES * HALF
SLAB = ENC_PAD // HD * HALF
REQ = 12
HB = 4


def ring_pairs(segments, turn, along_x_core):
    pairs = []
    for seg in range(segments):
        for place in range(RING):
            x, y = divmod(place, SIDE)
            if seg % 2 == along_x_core:
                to = ((x + turn) % SIDE) * SIDE + y
            else:
                to = x * SIDE + (y + turn) % SIDE
            pairs.append((seg * RING + place, seg * RING + to))
    return pairs


def ring_groups(segments, along_x_core):
    groups = []
    for seg in range(segments):
        for line in range(SIDE):
            if seg % 2 == along_x_core:
                groups.append([seg * RING + x * SIDE + line for x in range(SIDE)])
            else:
                groups.append([seg * RING + line * SIDE + y for y in range(SIDE)])
    return groups


def turned(value, turn, along_x_core):
    pairs = ring_pairs(lax.axis_size("segment"), turn, along_x_core)
    return lax.ppermute(value, ("segment", "db"), pairs)


def to_next_turned(value, turn):
    count = lax.axis_size("segment")
    behind = ring_pairs(count, turn, 0)
    pairs = [(((seg - 1) % count) * RING + place, to) for seg in range(count) for place, to in
             [(source % RING, target) for source, target in behind[seg * RING:(seg + 1) * RING]]]
    return lax.ppermute(value, ("segment", "db"), pairs)


def to_next(value):
    count = lax.axis_size("segment")
    return lax.ppermute(value, "segment", [(s, (s + 1) % count) for s in range(count)])


def to_next_other_mp(value):
    count = lax.axis_size("segment")
    pairs = [(s * 2 + m, ((s + 1) % count) * 2 + 1 - m) for s in range(count) for m in range(2)]
    return lax.ppermute(value, ("segment", "mp"), pairs)


def other_core(value):
    count = lax.axis_size("segment")
    return lax.ppermute(value, "segment", [(s, s ^ 1) for s in range(count)])


def fetch(table, first, sources, slabs, sems):
    def begin(i, carry):
        which = table[0, first + i]
        row = pl.multiple_of(table[1, first + i], 64)
        for number, source in enumerate(sources):
            @pl.when(which == number)
            def _():
                pltpu.make_async_copy(source.at[pl.ds(row, SLAB)], slabs.at[i], sems.at[i]).start()
        return carry

    def finish(i, carry):
        pltpu.make_async_copy(sources[0].at[pl.ds(0, SLAB)], slabs.at[i], sems.at[i]).wait()
        return carry

    lax.fori_loop(0, REQ, begin, 0)
    lax.fori_loop(0, REQ, finish, 0)


def spread_slabs(table, slabs, spread):
    tiles = ENC_PAD // HD
    rows = []
    for i in range(REQ):
        slab = slabs[i]
        even = jnp.concatenate([slab[t * HALF:(t + 1) * HALF] for t in range(tiles)], axis=1)
        odd = jnp.concatenate([even[:, SHIFT:], even[:, :SHIFT]], axis=1)
        rows.append(jnp.where(table[2, i] == 1, odd, even))
    stacked = jnp.concatenate(rows, axis=0)
    return jnp.dot(stacked, spread[...], preferred_element_type=jnp.float32).astype(jnp.bfloat16)


def give_kernel(table, c_ref, r_ref, ol_ref, or_ref, l_ref, out_ref, sems):
    fetch(table, REQ, (c_ref, r_ref, ol_ref, or_ref, l_ref), out_ref, sems)


def pick_kernel(table, c_ref, r_ref, ol_ref, or_ref, l_ref, spread, out_ref, slabs, sems):
    fetch(table, 0, (c_ref, r_ref, ol_ref, or_ref, l_ref), slabs, sems)
    out_ref[...] = spread_slabs(table, slabs, spread)


SMEM = pl.BlockSpec(memory_space=pltpu.SMEM)
VMEM = pl.BlockSpec(memory_space=pltpu.VMEM)
ANY = pl.BlockSpec(memory_space=pl.ANY)


def give(table, pieces):
    return pl.pallas_call(
        give_kernel,
        in_specs=[SMEM] + [ANY] * 5,
        out_specs=VMEM,
        out_shape=jax.ShapeDtypeStruct((REQ, SLAB, HD), jnp.bfloat16),
        scratch_shapes=[pltpu.SemaphoreType.DMA((REQ,))],
        compiler_params=pltpu.CompilerParams(vmem_limit_bytes=16 * 2**20),
        name="give_encodings",
    )(table, *pieces)


def pick(table, pieces, spread):
    return pl.pallas_call(
        pick_kernel,
        in_specs=[SMEM] + [ANY] * 5 + [VMEM],
        out_specs=VMEM,
        out_shape=jax.ShapeDtypeStruct((REQ * HALF, ENC_PAD), jnp.bfloat16),
        scratch_shapes=[
            pltpu.VMEM((REQ, SLAB, HD), jnp.bfloat16),
            pltpu.SemaphoreType.DMA((REQ,)),
        ],
        compiler_params=pltpu.CompilerParams(vmem_limit_bytes=32 * 2**20),
        name="pick_encodings",
    )(table, *pieces, spread)


def attend_kernel(
    live, table, own_ref, slabs, spread, w_ref, x_ref, inv_ref, gain_ref, out_ref, other_ref
):

    @pl.when(pl.program_id(0) == 0)
    def _():
        other_ref[...] = spread_slabs(table, slabs, spread)

    own, other = own_ref[...], other_ref[...]
    inv = inv_ref[...]
    groups = x_ref.shape[0] // GROUP
    column = lax.broadcasted_iota(jnp.int32, (1, HD), 1)
    biases = []
    for c in range(groups):
        bias = jnp.where(jnp.where(column < HALF, live[2 * c], live[2 * c + 1]) > 0, 0.0, -1e30)
        biases.append(jnp.broadcast_to(jnp.concatenate([bias, bias], axis=1), (GROUP, 4 * HALF)))
    bias = jnp.concatenate(biases, axis=0)
    for b in range(HB):
        base = b * 2 * W_PAD
        head = slice(b * HD, (b + 1) * HD)
        key_w = jnp.concatenate([w_ref[j, base:base + W_PAD] for j in range(RING)], axis=0)
        value_w = jnp.concatenate([w_ref[j, base + W_PAD:base + 2 * W_PAD] for j in range(RING)], axis=0)
        weight = jnp.concatenate([key_w, value_w], axis=1)
        kv_own = jnp.dot(own, weight, preferred_element_type=jnp.float32).astype(jnp.bfloat16)
        kv_other = jnp.dot(other, weight, preferred_element_type=jnp.float32).astype(jnp.bfloat16)
        x = x_ref[:, head].astype(jnp.float32)
        q = (x * inv * gain_ref[:, head] * HD ** (-0.5)).astype(jnp.bfloat16)
        scores, values = [], []
        for c in range(groups):
            keys = slice(c * 2 * HALF, (c + 1) * 2 * HALF)
            key = jnp.concatenate([kv_own[keys, :HD], kv_other[keys, :HD]], axis=0)
            values.append(jnp.concatenate([kv_own[keys, HD:], kv_other[keys, HD:]], axis=0))
            scores.append(
                lax.dot_general(
                    q[c * GROUP:(c + 1) * GROUP],
                    key,
                    (((1,), (1,)), ((), ())),
                    preferred_element_type=jnp.float32,
                )
            )
        masked = jnp.concatenate(scores, axis=0) + bias
        row_max = jnp.max(masked, axis=1, keepdims=True)
        row_max = jnp.where(row_max > -1e29, row_max, 0.0)
        expo = jnp.exp(masked - row_max)
        total = jnp.maximum(jnp.sum(expo, axis=1, keepdims=True), 1.0)
        probs = (expo * (1.0 / total)).astype(jnp.bfloat16)
        attended = [
            jnp.dot(probs[c * GROUP:(c + 1) * GROUP], values[c], preferred_element_type=jnp.float32)
            for c in range(groups)
        ]
        out_ref[:, head] = (x + jnp.concatenate(attended, axis=0)).astype(jnp.bfloat16)


def attend(live, table, own, slabs, spread, weights, x, inv, gain):
    tokens, width = x.shape
    whole = lambda *shape: pl.BlockSpec(shape, lambda i, live, table: (0,) * len(shape))
    return pl.pallas_call(
        attend_kernel,
        grid_spec=pltpu.PrefetchScalarGridSpec(
            num_scalar_prefetch=2,
            grid=(HEADS_HERE // HB,),
            in_specs=[
                whole(REQ * HALF, ENC_PAD),
                whole(REQ, SLAB, HD),
                whole(ENC_PAD, ENC_PAD),
                pl.BlockSpec((RING, HB * 2 * W_PAD, HD), lambda i, live, table: (0, i, 0)),
                pl.BlockSpec((tokens, HB * HD), lambda i, live, table: (0, i)),
                whole(tokens, 1),
                pl.BlockSpec((1, HB * HD), lambda i, live, table: (0, i)),
            ],
            out_specs=pl.BlockSpec((tokens, HB * HD), lambda i, live, table: (0, i)),
            scratch_shapes=[pltpu.VMEM((REQ * HALF, ENC_PAD), jnp.bfloat16)],
        ),
        out_shape=jax.ShapeDtypeStruct((tokens, width), jnp.bfloat16),
        compiler_params=pltpu.CompilerParams(vmem_limit_bytes=58 * 2**20),
        name="attend_heads",
    )(live, table, own, slabs, spread, weights, x, inv, gain)


def ring_place(owner, core):
    x, y = owner // SIDE, owner % SIDE
    return jnp.where(core == 0, x, y), jnp.where(core == 0, y, x)


def spread_of(core, here):
    channel = jnp.arange(ENC_PAD)
    near, far = ring_place(channel // W_PART, core)
    near = (near - ring_place(here, core)[0]) % SIDE
    place = (far * SIDE + near) * W_PAD + channel % W_PART
    place = lax.optimization_barrier(jnp.where(channel < ENC, place, -1))
    column = lax.broadcasted_iota(jnp.int32, (ENC_PAD, ENC_PAD), 1)
    return (place[:, None] == column).astype(jnp.bfloat16)


def source_table(requests, core, here):
    owner, block = requests // 6, requests % 6
    near, far = ring_place(owner, core)
    far = (far - ring_place(here, core)[1]) % SIDE
    which = jnp.where(far < 2, far, jnp.where(far == 3, 4, jnp.where(near < 2, 2, 3)))
    chunk = jnp.where(which == 3, near - 2, near)
    odd = block % 2
    row = chunk * D_ROWS + (block // 2) * (TILES * HALF) + odd * (TILES - ENC_PAD // HD) * HALF
    return jnp.stack([which, row, odd])


def first_ring(piece):
    groups = ring_groups(lax.axis_size("segment"), 0)
    copies = jnp.tile(piece, (SIDE, 1))
    return lax.all_to_all(
        copies, ("segment", "db"), split_axis=0, concat_axis=0, tiled=True, axis_index_groups=groups
    )


def on_device(stream, gain, key_weight, value_weight, owners, blocks, valid, database):
    core = lax.axis_index("segment") % 2
    place = lax.axis_index("db")
    rows = stream[0]
    tokens, local_width = rows.shape
    full_width = local_width * lax.axis_size("mp")

    def pack_weight(w):
        return jnp.pad(w[0], ((0, W_PAD - W_PART), (0, 0)))

    packed_w = jnp.concatenate([pack_weight(key_weight), pack_weight(value_weight)], axis=0)
    packed_w = packed_w.reshape(2 * W_PAD, HEADS_HERE, HD).transpose(1, 0, 2).reshape(W_ROWS, HD)

    half = lax.dynamic_slice(database, (0, core * HALF, 0), (2 * PAIRS, HALF, ENC))
    paired = jnp.concatenate([half[0::2], half[1::2]], axis=2)
    packed_d = paired.reshape(PAIRS, HALF, TILES, HD).transpose(0, 2, 1, 3).reshape(D_ROWS, HD)

    as_float = rows.astype(jnp.float32)
    squares = jnp.sum(as_float * as_float, axis=1)
    requests = (owners[0] * 6 + blocks[0]).reshape(-1)
    info = jnp.concatenate(
        [squares, gain[0], valid[0].reshape(-1).astype(jnp.float32), requests.astype(jnp.float32)]
    )
    info = jnp.pad(info, (0, -info.shape[0] % 1024)).reshape(-1, HD)

    pieces_w = [to_next_turned(packed_w, turn) for turn in (0, -1, 2, 1)]
    pieces_w[0], line_d, info, squares = lax.optimization_barrier(
        (pieces_w[0], first_ring(packed_d), info, squares)
    )
    all_w = lax.all_gather(
        jnp.concatenate(pieces_w, axis=0),
        ("segment", "db"),
        axis=0,
        tiled=True,
        axis_index_groups=ring_groups(lax.axis_size("segment"), 1),
    ).reshape(RING, W_ROWS, HD)
    d_before, d_after = turned(line_d, 1, 1), turned(line_d, -1, 1)
    info_here = to_next(info).reshape(-1)
    squares_here = info_here[:tokens]
    gain_here = info_here[tokens:tokens + local_width]
    ints = info_here[tokens + local_width:tokens + local_width + 2 * REQ].astype(jnp.int32)
    live, requests_here = ints[:REQ], ints[REQ:]
    requests_other = other_core(requests_here)
    spread = spread_of(core, place)
    squares_other = to_next_other_mp(squares.reshape(-1, HD)).reshape(-1)
    d_before, d_after, spread, requests_other, squares_other, rows = lax.optimization_barrier(
        (d_before, d_after, spread, requests_other, squares_other, rows)
    )
    x_here = to_next(rows)
    mid_d = line_d.shape[0] // 2
    d_pieces = (line_d, d_after, turned(d_before[:mid_d], 1, 1), turned(d_after[mid_d:], -1, 1), d_before)

    table = jnp.concatenate(
        [source_table(requests_here, core, place), source_table(requests_other, core, place)], axis=1
    )

    inv_rms = lax.rsqrt((squares_here + squares_other) / full_width + eps_norm)
    slabs = other_core(give(table, d_pieces))
    own_table, x_here, inv_column, gain_row = lax.optimization_barrier(
        (table, x_here, inv_rms[:, None], gain_here[None, :])
    )
    own = pick(own_table, d_pieces, spread)
    updated = attend(live, table, own, slabs, spread, all_w, x_here, inv_column, gain_row)
    return updated[None]


def solution(mesh):
    return jax.shard_map(
        on_device,
        mesh=mesh,
        in_specs=(
            P("segment", "db", "mp"),
            P("segment", "mp"),
            P("segment", "db", "mp"),
            P("segment", "db", "mp"),
            P("segment", "db", None),
            P("segment", "db", None),
            P("segment", "db", None),
            P("db", None, None),
        ),
        out_specs=P("segment", "db", "mp"),
        check_vma=False,
    )
```
